32 devices in a mesh: chan: 16 (over z, y, core), loc: 2 (over x).
Axes of the slice: x: 2, y: 2, z: 4, core: 2. Of those that a mesh axis runs over, the one named last changes fastest.
Arguments:
- pixels: bfloat16 [512, 256, 256], P('loc', 'chan'), may hold values from -6 to 6
- patch_mask: int32 [512, 256], P('loc', 'chan'), may hold values 0 or 1
- group_map: int32 [256], replicated, may hold values from 0 to 63, as said below
- embed_weight: bfloat16 [256, 2048], P(None, 'loc'), may hold values from -0.375 to 0.375
- mask_token: bfloat16 [2048], replicated, may hold values from -6 to 6
- chan_embed: bfloat16 [256, 2048], P('chan'), may hold values from -3 to 3
- agg_weight: float32 [256], P('chan'), may hold values from 0.5 to 2
- query_key: bfloat16 [16, 2048], replicated, may hold values from -0.02734375 to 0.02734375
- group_bias: float32 [16, 64], replicated, may hold values from -0.5 to 255
- norm_gain: float32 [2048], replicated, may hold values from 0.25 to 1.75
- head_weight: bfloat16 [2048, 256, 256], P(None, 'chan'), may hold values from -0.125 to 0.125
- head_bias: float32 [256, 256], P('chan'), may hold values from -3 to 3
Outputs:
- rebuilt: bfloat16 [512, 256, 256], P('loc', 'chan')
The draws below stay inside these ranges and needn't reach their ends.
Inputs may be any that keep to these rules, and one draw needn't show every extreme that they name: `group_map`: the 4 channels of each bundle (channels k * 4 to k * 4 + 3) name at most two distinct groups.
All inputs are finite; a program needn't handle non-finite values. No bound on the sum of `patch_mask` on one device may be relied on, other than what follows from the above.
Results may differ from the reference program's by a relative error of at most 0.0051.
Values may be sent and summed in bfloat16 or wider, within the bound.
No kernel may reach another device: no remote copies, remote signals or barrier semaphores. Data moves between devices by JAX's collectives and lax.ppermute only.
A program may use at most 128 MiB of HBM per device.

```python
import math
import jax
import jax.numpy as jnp
from jax import lax

C = 256
E = 2048
P_SIZE = 256
G = 64
H = 16
BUNDLE = 4
LOCS = 512


def draw_group_map(key, part):
    bundles = C // BUNDLE
    key_first, key_shift, key_pick = jax.random.split(jax.random.fold_in(key, 11), 3)
    first_group = jax.random.randint(key_first, (bundles,), 0, G)
    second_group = (first_group + jax.random.randint(key_shift, (bundles,), 1, G)) % G
    picked = jax.random.randint(key_pick, (bundles, BUNDLE), 0, 2)
    leading = jnp.arange(BUNDLE)[None, :] == 0
    picked = jnp.where(leading, 0, picked)
    groups = jnp.where(picked == 1, second_group[:, None], first_group[:, None])
    return groups.reshape(C).astype(jnp.int32)


def draw_group_bias(key, part):
    key_base, key_top, key_amount = jax.random.split(jax.random.fold_in(key, 23), 3)
    baseline = jax.random.uniform(key_base, (H, G), jnp.float32, -0.5, 0.5)
    top_group = jax.random.randint(key_top, (H,), 0, G)
    amount = jax.random.uniform(key_amount, (H,), jnp.float32, 2.0, 4.0)
    group_ids = jnp.arange(G)[None, :]
    on_top = group_ids == top_group[:, None]
    biased = baseline + jnp.where(on_top, amount[:, None], 0.0)
    return biased.astype(jnp.float32)


def touch_ends(values, stream_key, least, high):
    shape = values.shape
    index_at = [jax.random.randint(jax.random.fold_in(stream_key, axis), (), 0, shape[axis]) for axis in range(len(shape))]
    values = values.at[tuple(index_at)].set(least)
    longest = shape.index(max(shape))
    index_at[longest] = (index_at[longest] + 1) % shape[longest]
    return values.at[tuple(index_at)].set(high)


def block_levels(stream_key, shape, cuts, least, largest):
    gain, own = 1.0, jax.random.fold_in(stream_key, 6)
    for position, blocks in cuts:
        steps = jnp.exp(jax.random.uniform(jax.random.fold_in(own, position), (blocks,), jnp.float32, least / len(cuts), largest / len(cuts)))
        gain = gain * jnp.repeat(steps, shape[position] // blocks).reshape([-1 if axis == position else 1 for axis in range(len(shape))])
    return gain


def normal_values(stream_key, extent, width, bound, cuts=(), kind=jnp.bfloat16):
    array = jax.random.normal(stream_key, extent, jnp.float32) * width
    if len(cuts) > 0:
        array = block_levels(stream_key, extent, cuts, -0.22, 0.18) * array
    return jnp.clip(array, min=-bound, max=bound).astype(kind)


def setup_inputs(seed: int = 0) -> dict:
    key_list = jax.random.split(jax.random.key(seed), 13)
    pixels = normal_values(key_list[0], (LOCS, C, P_SIZE), 1.0, 6.0, ((0, 2), (1, 16)))
    patch_mask = touch_ends((jax.random.randint(key_list[1], (LOCS, C), 0, 4) < 3).astype(jnp.int32), jax.random.fold_in(key_list[1], 1), 0, 1)
    group_map = draw_group_map(jax.random.fold_in(key_list[12], 71), 0)
    embed_weight = normal_values(key_list[3], (P_SIZE, E), P_SIZE ** -0.5, 0.375, ((1, 2),))
    mask_token = normal_values(key_list[4], (E,), 1.0, 6.0)
    chan_embed = normal_values(key_list[5], (C, E), 0.5, 3.0, ((0, 16),))
    agg_weight = jnp.clip(jnp.exp(math.log(2.0) - 1.3862944 * jax.random.uniform(key_list[6], (C,), jnp.float32) ** block_levels(key_list[6], (C,), ((0, 16),), -0.2, 0.2)), 0.5, 2.0)
    query_key = normal_values(key_list[7], (H, E), (25 * E) ** -0.5, 0.02734375)
    group_bias = draw_group_bias(jax.random.fold_in(key_list[12], 71), 0)
    norm_gain = jnp.clip(1.0 + 0.15 * jax.random.normal(key_list[9], (E,), jnp.float32), 0.25, 1.75)
    head_weight = normal_values(key_list[10], (E, C, P_SIZE), E ** -0.5, 0.125, ((1, 16),))
    head_bias = normal_values(key_list[11], (C, P_SIZE), 0.5, 3.0, ((0, 16),), jnp.float32)
    return {"pixels": pixels, "patch_mask": patch_mask, "group_map": group_map, "embed_weight": embed_weight, "mask_token": mask_token, "chan_embed": chan_embed, "agg_weight": agg_weight, "query_key": query_key, "group_bias": group_bias, "norm_gain": norm_gain, "head_weight": head_weight, "head_bias": head_bias}


def slot_tables(group_map):
    bundled = group_map.reshape(C // BUNDLE, BUNDLE)
    lowest = lax.optimization_barrier(jnp.min(bundled, axis=1))
    highest = lax.optimization_barrier(jnp.max(bundled, axis=1))
    slot_index = (bundled != lowest[:, None]).astype(jnp.int32)
    choose = slot_index[:, None, :] == jnp.arange(2, dtype=jnp.int32)[None, :, None]
    slot_group = jnp.stack([lowest, highest], axis=1).reshape(C // 2)
    to_group = jnp.arange(G, dtype=jnp.int32)[:, None] == slot_group[None, :]
    return (choose, to_group)

def attend(aggregate, query_key, group_bias, norm_gain):
    row_count = aggregate.shape[0]
    scores = jnp.einsum('lge,he->lhg', aggregate, query_key.astype(jnp.float32), precision=lax.Precision.HIGHEST) + group_bias[None]
    weights = jax.nn.softmax(scores, axis=-1)
    pooled = jnp.einsum('lhg,lghd->lhd', weights, aggregate.reshape(row_count, G, H, E // H), precision=lax.Precision.HIGHEST).reshape(row_count, E)
    inverse_rms = lax.rsqrt(lax.optimization_barrier(jnp.mean(pooled * pooled, axis=-1, keepdims=True)) + 1e-06)
    return (pooled * inverse_rms * norm_gain[None]).astype(jnp.bfloat16)

def reference(pixels, patch_mask, group_map, embed_weight, mask_token, chan_embed, agg_weight, query_key, group_bias, norm_gain, head_weight, head_bias):
    choose, to_group = slot_tables(group_map)
    flat_heads = head_weight.reshape(E, C * P_SIZE)
    flat_bias = head_bias.reshape(1, C * P_SIZE).astype(jnp.float32)
    block_rows = 64

    def location_block(inputs):
        block_pixels, block_mask = inputs
        projected = jnp.dot(block_pixels.reshape(block_rows * C, P_SIZE), embed_weight, preferred_element_type=jnp.float32).reshape(block_rows, C, E)
        pre_act = jnp.where(block_mask[:, :, None] == 1, mask_token.astype(jnp.float32)[None, None, :], projected) + chan_embed.astype(jnp.float32)[None]
        weighted = (jax.nn.gelu(pre_act, approximate=False) * agg_weight[None, :, None]).astype(jnp.bfloat16)
        bundle_sums = jnp.einsum('lbke,bsk->lbse', weighted.reshape(block_rows, C // BUNDLE, BUNDLE, E).astype(jnp.float32), choose.astype(jnp.float32), precision=lax.Precision.HIGHEST)
        bundle_sums = bundle_sums.reshape(block_rows, C // 2, E).astype(jnp.bfloat16)
        aggregate = jnp.einsum('gq,lqe->lge', to_group.astype(jnp.float32), bundle_sums.astype(jnp.float32), precision=lax.Precision.HIGHEST)
        joined_tokens = attend(aggregate, query_key, group_bias, norm_gain)
        decoded = jnp.dot(joined_tokens, flat_heads, preferred_element_type=jnp.float32) + flat_bias
        return decoded.astype(jnp.bfloat16).reshape(block_rows, C, P_SIZE)
    blocks = LOCS // block_rows
    rebuilt = lax.map(location_block, (pixels.reshape(blocks, block_rows, C, P_SIZE), patch_mask.reshape(blocks, block_rows, C)))
    return rebuilt.reshape(LOCS, C, P_SIZE)
```

```python
import functools

import jax
import jax.numpy as jnp
from jax import lax
from jax.experimental import pallas as pl
from jax.experimental.pallas import tpu as pltpu
from jax.sharding import PartitionSpec as P

G = 64
BUNDLE = 4
LANES = 128
VMEM = pl.BlockSpec(memory_space=pltpu.VMEM)
ANY = pl.BlockSpec(memory_space=pl.ANY)
F32, BF16 = jnp.float32, jnp.bfloat16


def dot(left, right, left_dim=1, right_dim=0):
    dims = (((left_dim,), (right_dim,)), ((), ()))
    return lax.dot_general(left, right, dims, preferred_element_type=F32)


def iota(shape, axis):
    return lax.broadcasted_iota(jnp.int32, shape, axis)


def halves(value):
    high = value.astype(BF16)
    return high, (value - high.astype(F32)).astype(BF16)


def gelu(value):
    return 0.5 * value * (1.0 + lax.erf(value * 0.7071067811865476))


def slot_tables(group_map):
    bundled = group_map.reshape(-1, BUNDLE)
    lowest = jnp.min(bundled, axis=1)
    highest = jnp.max(bundled, axis=1)
    slot_index = (bundled != lowest[:, None]).astype(jnp.int32)
    choose = slot_index[:, None, :] == jnp.arange(2, dtype=jnp.int32)[None, :, None]
    slot_group = jnp.stack([lowest, highest], axis=1).reshape(-1)
    to_group = jnp.arange(G, dtype=jnp.int32)[:, None] == slot_group[None, :]
    return (choose.astype(BF16), to_group.astype(BF16))


def attend(aggregate, query_key, group_bias, norm_gain):
    rows, _, features = aggregate.shape
    heads = query_key.shape[0]
    high = lax.Precision.HIGHEST
    scores = jnp.einsum("lge,he->lhg", aggregate, query_key.astype(F32), precision=high)
    weights = jax.nn.softmax(scores + group_bias[None], axis=-1)
    split = aggregate.reshape(rows, G, heads, features // heads)
    pooled = jnp.einsum("lhg,lghd->lhd", weights, split, precision=high).reshape(rows, features)
    inverse_rms = lax.rsqrt(jnp.mean(pooled * pooled, axis=-1, keepdims=True) + 1e-06)
    return (pooled * inverse_rms * norm_gain[None]).astype(BF16)


def plain_join(
    pixels, patch_mask, group_map, embed_weight, mask_token, chan_embed, agg_weight, query_key, group_bias, norm_gain
):
    pixel_count = pixels.shape[2]
    choose, to_group = slot_tables(group_map)
    source_pixels = lax.all_to_all(pixels, "chan", split_axis=0, concat_axis=1, tiled=True)
    source_mask = lax.all_to_all(patch_mask, "chan", split_axis=0, concat_axis=1, tiled=True)
    offsets = lax.all_gather(chan_embed, "chan", axis=0, tiled=True).astype(F32)
    weights = lax.all_gather(agg_weight, "chan", axis=0, tiled=True)
    section = lax.all_gather(embed_weight, "loc", axis=1, tiled=True)
    rows, channels, _ = source_pixels.shape
    features = section.shape[1]
    projected = jnp.dot(source_pixels.reshape(rows * channels, pixel_count), section, preferred_element_type=F32)
    projected = projected.reshape(rows, channels, features)
    hidden = source_mask.reshape(rows, channels, 1) == 1
    pre = jnp.where(hidden, mask_token.astype(F32)[None, None, :], projected) + offsets[None]
    weighted = (jax.nn.gelu(pre, approximate=False) * weights[None, :, None]).astype(BF16)
    bundled = weighted.reshape(rows, channels // BUNDLE, BUNDLE, features)
    sums = jnp.einsum("lbke,bsk->lbse", bundled, choose, preferred_element_type=F32)
    sums = sums.reshape(rows, channels // BUNDLE * 2, features).astype(BF16)
    aggregate = jnp.einsum("gq,lqe->lge", to_group, sums, preferred_element_type=F32)
    return attend(aggregate, query_key, group_bias, norm_gain)


def plain_shards(
    pixels,
    patch_mask,
    group_map,
    embed_weight,
    mask_token,
    chan_embed,
    agg_weight,
    query_key,
    group_bias,
    norm_gain,
    head_weight,
    head_bias,
):
    _, own_channels, pixel_count = pixels.shape
    joined = plain_join(
        pixels, patch_mask, group_map, embed_weight, mask_token, chan_embed, agg_weight, query_key, group_bias, norm_gain
    )
    section = lax.all_gather(joined, "chan", axis=0, tiled=True)
    flat_heads = head_weight.reshape(-1, own_channels * pixel_count)
    decoded = jnp.dot(section, flat_heads, preferred_element_type=F32) + head_bias.reshape(1, -1)
    return decoded.astype(BF16).reshape(section.shape[0], own_channels, pixel_count)


def pack_kernel(rows, pixels_ref, mask_ref, weight_ref, out_ref):
    peers, pair_rows, width = pixels_ref.shape
    own, locations = mask_ref.shape
    per = locations // peers
    spread = (iota((own, pair_rows), 1) % own == iota((own, pair_rows), 0)).astype(BF16)
    by_location = dot(mask_ref[...].astype(F32).astype(BF16), spread, 0, 0)
    by_location = by_location.reshape(peers, per, pair_rows)
    keep = iota((1, per, pair_rows), 2) // own == iota((1, per, pair_rows), 1)
    hidden = jnp.sum(jnp.where(keep, by_location, 0.0), axis=1)
    visible = 1.0 - hidden
    before = (iota((pair_rows, pair_rows), 0) < iota((pair_rows, pair_rows), 1)).astype(BF16)
    rank = dot(visible.astype(BF16), before)
    place = jnp.where(visible > 0.5, rank, -1.0)
    limit = float(rows - 2)
    over = jnp.max(place, keepdims=True) >= limit
    marked = hidden + jnp.where(over, 2.0, 0.0)
    weight = weight_ref[...]
    high = weight.astype(BF16)
    middle = (weight - high.astype(F32)).astype(BF16)
    low = (weight - high.astype(F32) - middle.astype(F32)).astype(BF16)
    lane = iota((own, width), 1)
    line = iota((own, width), 0)
    weight_row = jnp.zeros((1, width), F32)
    for part, value in enumerate((high, middle, low)):
        weight_row += dot(value, (lane == line + part * own).astype(BF16))
    index = iota((rows, pair_rows), 0).astype(F32)
    for peer in range(peers):
        chosen = (place[peer : peer + 1, :] == index).astype(BF16)
        packed = dot(chosen, pixels_ref[peer])
        line = iota((rows, width), 0)
        mask_row = jnp.pad(marked[peer : peer + 1, :], ((0, 0), (0, width - pair_rows)))
        packed = jnp.where(line == rows - 2, weight_row, packed)
        packed = jnp.where(line == rows - 1, mask_row, packed)
        out_ref[peer] = packed.astype(BF16)


def join_kernel(
    sizes,
    place_ref,
    packed_ref,
    *refs,
):
    sources, own, per, heads, chunk = sizes
    section_refs = refs[: sizes_sections(refs)]
    rest = refs[len(section_refs) :]
    (chan_ref, other_ref, token_ref, query_ref, group_ref, bias_ref, gain_ref, out_ref) = rest[:8]
    (embed, offset, table, choice, where, value, score) = rest[8:]
    _, rows, width = packed_ref.shape
    total = sources * rows
    features = embed.shape[1]
    channels = sources * own
    pair_rows = per * own
    depth = features // heads
    chunks = total // chunk

    me_loc = place_ref[0]
    me = place_ref[1]
    sections = len(section_refs)
    part = features // sections
    for step, section in enumerate(section_refs):
        at = lax.rem(me_loc + step, sections) * part
        embed[:, pl.ds(pl.multiple_of(at, part), part)] = section[...]
    half = sources // 2
    for step in range(half):
        for ref, flip in ((chan_ref, 0), (other_ref, 1)):
            source = jnp.bitwise_xor(me, 2 * step + flip)
            offset[pl.ds(pl.multiple_of(source * own, own), own), :] = ref[step * own : (step + 1) * own, :]

    last = [packed_ref[s, rows - 16 :, :].astype(F32) for s in range(sources)]
    marked = jnp.concatenate([tail[15:16, :] for tail in last], axis=0)[:, :pair_rows]
    weight_rows = jnp.concatenate([tail[14:15, :] for tail in last], axis=0)
    hidden = jnp.where(marked >= 2.0, marked - 2.0, marked)
    visible = 1.0 - hidden
    before = (iota((pair_rows, pair_rows), 0) < iota((pair_rows, pair_rows), 1)).astype(BF16)
    rank = dot(visible.astype(BF16), before)
    place = jnp.where(visible > 0.5, rank, -1.0)
    index = iota((rows, pair_rows), 0).astype(F32)
    of_row = iota((pair_rows, LANES), 0) // own
    to_location = (of_row == iota((pair_rows, LANES), 1)).astype(BF16)
    channel_of_row = iota((pair_rows, channels), 0) % own
    for s in range(sources):
        chosen = (place[s : s + 1, :] == index).astype(BF16)
        to_channel = (channel_of_row + s * own == iota((pair_rows, channels), 1)).astype(BF16)
        choice[s * rows : (s + 1) * rows, :] = dot(chosen, to_channel).astype(BF16)
        where[s * rows : (s + 1) * rows, :] = dot(chosen, to_location).astype(BF16)
    lane = iota((width, channels), 0)
    spread = ((lane % own == iota((width, channels), 1) % own) & (lane < 3 * own)).astype(BF16)
    each = dot(weight_rows.astype(BF16), spread)
    mine = iota((sources, channels), 1) // own == iota((sources, channels), 0)
    weight = jnp.sum(jnp.where(mine, each, 0.0), axis=0, keepdims=True)

    block = 256
    for at in range(0, features, block):
        cols = slice(at, at + block)
        table[:, cols] = gelu(token_ref[:, cols].astype(F32) + offset[:, cols].astype(F32)).astype(BF16)
    table_score = dot(query_ref[...], table[...], 1, 1)

    eye = (iota((per, LANES), 0) == iota((per, LANES), 1)).astype(BF16)
    tile = 128
    counts = jnp.zeros((per, channels), F32)
    spread_score = jnp.zeros((heads * per, channels), F32)
    for c in range(chunks):
        base = c * chunk
        for at in range(0, features, block):
            cols = slice(at, at + block)
            for top in range(base, base + chunk, tile):
                line = slice(top, top + tile)
                pixel = packed_ref[...].reshape(total, width)[line, :]
                pre = dot(pixel, embed[:, cols]) + dot(choice[line, :], offset[:, cols])
                value[line, cols] = gelu(pre).astype(BF16)
        line = slice(base, base + chunk)
        score[c] = dot(query_ref[...], value[line, :], 1, 1)
        at_location = dot(eye, where[line, :], 1, 1)
        counts += dot(at_location.astype(BF16), choice[line, :])
        by_row = [score[c, h : h + 1, :] * at_location for h in range(heads)]
        for piece in halves(jnp.concatenate(by_row, axis=0)):
            spread_score += dot(piece, choice[line, :])

    hidden_at = 1.0 - counts
    by_row = [hidden_at * table_score[h : h + 1, :] for h in range(heads)]
    full = (spread_score + jnp.concatenate(by_row, axis=0)) * weight
    groups = bias_ref.shape[1]
    to_group = (iota((groups, channels), 0) == group_ref[...]).astype(BF16)
    scores = sum(dot(piece, to_group, 1, 1) for piece in halves(full))
    scores += jnp.concatenate([jnp.broadcast_to(bias_ref[h : h + 1, :], (per, groups)) for h in range(heads)], axis=0)
    scores = jnp.exp(scores - jnp.max(scores, axis=-1, keepdims=True))
    attention = scores / jnp.sum(scores, axis=-1, keepdims=True)
    each = sum(dot(piece, to_group) for piece in halves(attention)) * weight

    of_table = halves(each * jnp.concatenate([hidden_at] * heads, axis=0))
    each = halves(each)
    pooled = [jnp.zeros((2 * per, depth), F32)] * heads

    def stack(pieces, h):
        return jnp.concatenate([piece[h * per : (h + 1) * per, :] for piece in pieces], axis=0)

    for h in range(heads):
        pooled[h] += dot(stack(of_table, h), table[:, h * depth : (h + 1) * depth])
    for c in range(chunks):
        line = slice(c * chunk, (c + 1) * chunk)
        at_location = dot(eye, where[line, :], 1, 1)
        spread_each = sum(dot(piece, choice[line, :], 1, 1) for piece in each)
        pieces = halves(spread_each * jnp.concatenate([at_location] * heads, axis=0))
        for h in range(heads):
            pooled[h] += dot(stack(pieces, h), value[line, h * depth : (h + 1) * depth])
    pooled = [both[:per] + both[per:] for both in pooled]
    square = sum(jnp.sum(rows_of * rows_of, axis=-1, keepdims=True) for rows_of in pooled)
    scale = lax.rsqrt(square * (1.0 / features) + 1e-06)
    for h in range(heads):
        cols = slice(h * depth, (h + 1) * depth)
        out_ref[:, cols] = (pooled[h] * scale * gain_ref[:, cols]).astype(BF16)


def sizes_sections(refs):
    return len(refs) - 15


def decode_kernel(place_ref, near_ref, far_ref, head_ref, bias_ref, out_ref, heads, line, arrived):
    own = bias_ref.shape[0]
    half = near_ref.shape[0]
    per = out_ref.shape[1]
    me = place_ref[1]
    copies = [pltpu.make_async_copy(head_ref.at[c], heads.at[c], arrived.at[c]) for c in range(own)]
    for copy in copies:
        copy.start()
    for c in range(own):
        copies[c].wait()
        for flip, ref in ((0, near_ref), (1, far_ref)):
            decoded = dot(ref[...], heads[c]) + bias_ref[c : c + 1, :]
            for step in range(half // per):
                owner = jnp.bitwise_xor(me, 2 * step + flip)
                line[owner, :, c, :] = decoded[step * per : (step + 1) * per, :]
    for owner in range(2 * half // per):
        out_ref[owner] = line[owner].astype(BF16)


def flipped(value, axis, count, flip):
    return lax.ppermute(value, axis, [(i, i ^ flip) for i in range(count)])


def spread_rows(value, axis, count):
    near = [value] + [flipped(value, axis, count, 2 * k) for k in range(1, count // 2)]
    near = jnp.concatenate(near, axis=0)
    return near, flipped(near, axis, count, 1)


def whole(value):
    return jax.ShapeDtypeStruct(value[0], value[1])


def shards(
    peers,
    blocks,
    pixels,
    patch_mask,
    group_map,
    embed_weight,
    mask_token,
    chan_embed,
    agg_weight,
    query_key,
    group_bias,
    norm_gain,
    head_weight,
    head_bias,
):
    locations, own, pixel_count = pixels.shape
    channels = group_map.shape[0]
    heads, features = query_key.shape
    per = locations // peers
    pair_rows = per * own
    rows = -(-pair_rows * 3 // 8 // 16) * 16
    total = peers * rows
    fits = (
        peers & (peers - 1) == 0
        and own % 16 == 0
        and per % 16 == 0
        and pair_rows <= pixel_count
        and 3 * own <= pixel_count
        and total % 512 == 0
    )
    if not fits:
        return plain_shards(
            pixels,
            patch_mask,
            group_map,
            embed_weight,
            mask_token,
            chan_embed,
            agg_weight,
            query_key,
            group_bias,
            norm_gain,
            head_weight,
            head_bias,
        )
    vmem = pltpu.CompilerParams(vmem_limit_bytes=48 << 20)
    place = jnp.stack([lax.axis_index("loc"), lax.axis_index("chan")]).astype(jnp.int32)

    packed = pl.pallas_call(
        functools.partial(pack_kernel, rows),
        out_shape=jax.ShapeDtypeStruct((peers, rows, pixel_count), BF16),
        in_specs=[VMEM] * 3,
        out_specs=VMEM,
        compiler_params=vmem,
        name="pack",
    )(pixels.reshape(peers, pair_rows, pixel_count), patch_mask.T, agg_weight.reshape(1, own))
    sections = [embed_weight]
    for step in range(1, blocks):
        hop = [(i, (i - step) % blocks) for i in range(blocks)]
        sections.append(lax.ppermute(embed_weight, "loc", hop))
    near, far = spread_rows(chan_embed, "chan", peers)
    packed = lax.all_to_all(packed, "chan", split_axis=0, concat_axis=0, tiled=True)

    over = jnp.max((packed[:, rows - 1, :LANES].astype(F32) >= 2.0).astype(jnp.int32))
    over = jnp.broadcast_to(over, (8, LANES))
    most = over
    for step in range(1, blocks):
        hop = [(i, (i - step) % blocks) for i in range(blocks)]
        most = jnp.maximum(most, lax.ppermute(over, "loc", hop))

    chunk = 512
    joined = pl.pallas_call(
        functools.partial(join_kernel, (peers, own, per, heads, chunk)),
        out_shape=jax.ShapeDtypeStruct((per, features), BF16),
        in_specs=[pl.BlockSpec(memory_space=pltpu.SMEM)] + [VMEM] * (8 + blocks),
        out_specs=VMEM,
        scratch_shapes=[
            pltpu.VMEM((pixel_count, features), BF16),
            pltpu.VMEM((channels, features), BF16),
            pltpu.VMEM((channels, features), BF16),
            pltpu.VMEM((total, channels), BF16),
            pltpu.VMEM((total, LANES), BF16),
            pltpu.VMEM((total, features), BF16),
            pltpu.VMEM((total // chunk, heads, chunk), F32),
        ],
        compiler_params=vmem,
        name="join",
    )(
        place,
        packed,
        *sections,
        near,
        far,
        mask_token.reshape(1, features),
        query_key,
        group_map.reshape(1, channels),
        group_bias,
        norm_gain.reshape(1, features),
    )
    joined = lax.cond(
        most[0, 0] > 0,
        lambda: plain_join(
            pixels,
            patch_mask,
            group_map,
            embed_weight,
            mask_token,
            chan_embed,
            agg_weight,
            query_key,
            group_bias,
            norm_gain,
        ),
        lambda: joined,
    )
    near, far = spread_rows(joined, "chan", peers)
    by_channel = jnp.transpose(head_weight, (1, 0, 2))
    rebuilt = pl.pallas_call(
        decode_kernel,
        out_shape=jax.ShapeDtypeStruct((peers, per, own, pixel_count), BF16),
        in_specs=[pl.BlockSpec(memory_space=pltpu.SMEM), VMEM, VMEM, ANY, VMEM],
        out_specs=VMEM,
        scratch_shapes=[
            pltpu.VMEM((own, features, pixel_count), BF16),
            pltpu.VMEM((peers, per, own, pixel_count), F32),
            pltpu.SemaphoreType.DMA((own,)),
        ],
        compiler_params=vmem,
        name="decode",
    )(place, near, far, by_channel, head_bias)
    return rebuilt.reshape(locations, own, pixel_count)


def solution(mesh):
    return jax.shard_map(
        functools.partial(shards, mesh.shape["chan"], mesh.shape["loc"]),
        mesh=mesh,
        in_specs=(
            P("loc", "chan", None),
            P("loc", "chan"),
            P(),
            P(None, "loc"),
            P(),
            P("chan", None),
            P("chan"),
            P(),
            P(),
            P(),
            P(None, "chan", None),
            P("chan", None),
        ),
        out_specs=P("loc", "chan", None),
        check_vma=False,
    )
```

```python
import functools

import jax
import jax.numpy as jnp
from jax import lax
from jax.experimental import pallas as pl
from jax.experimental.pallas import tpu as pltpu
from jax.sharding import PartitionSpec as P

G = 64
BUNDLE = 4
LANES = 128
VMEM = pl.BlockSpec(memory_space=pltpu.VMEM)
SMEM = pl.BlockSpec(memory_space=pltpu.SMEM)
ANY = pl.BlockSpec(memory_space=pl.ANY)
F32, BF16 = jnp.float32, jnp.bfloat16


def dot(left, right, left_dim=1, right_dim=0):
    dims = (((left_dim,), (right_dim,)), ((), ()))
    return lax.dot_general(left, right, dims, preferred_element_type=F32)


def iota(shape, axis):
    return lax.broadcasted_iota(jnp.int32, shape, axis)


def halves(value):
    high = value.astype(BF16)
    return high, (value - high.astype(F32)).astype(BF16)


def gelu(value):
    return 0.5 * value * (1.0 + lax.erf(value * 0.7071067811865476))


def slot_tables(group_map):
    bundled = group_map.reshape(-1, BUNDLE)
    lowest = jnp.min(bundled, axis=1)
    highest = jnp.max(bundled, axis=1)
    slot_index = (bundled != lowest[:, None]).astype(jnp.int32)
    choose = slot_index[:, None, :] == jnp.arange(2, dtype=jnp.int32)[None, :, None]
    slot_group = jnp.stack([lowest, highest], axis=1).reshape(-1)
    to_group = jnp.arange(G, dtype=jnp.int32)[:, None] == slot_group[None, :]
    return (choose.astype(BF16), to_group.astype(BF16))


def attend(aggregate, query_key, group_bias, norm_gain):
    rows, _, features = aggregate.shape
    heads = query_key.shape[0]
    high = lax.Precision.HIGHEST
    scores = jnp.einsum("lge,he->lhg", aggregate, query_key.astype(F32), precision=high)
    weights = jax.nn.softmax(scores + group_bias[None], axis=-1)
    split = aggregate.reshape(rows, G, heads, features // heads)
    pooled = jnp.einsum("lhg,lghd->lhd", weights, split, precision=high).reshape(rows, features)
    inverse_rms = lax.rsqrt(jnp.mean(pooled * pooled, axis=-1, keepdims=True) + 1e-06)
    return (pooled * inverse_rms * norm_gain[None]).astype(BF16)


def gathered(value, axis, dim):
    count = lax.axis_size(axis)
    copies = jnp.broadcast_to(value[None], (count,) + value.shape)
    parts = lax.all_to_all(copies, axis, split_axis=0, concat_axis=0, tiled=True)
    parts = jnp.moveaxis(parts, 0, dim)
    return parts.reshape(value.shape[:dim] + (-1,) + value.shape[dim + 1 :])


def plain_join(
    pixels, patch_mask, group_map, embed_weight, mask_token, chan_embed, agg_weight, query_key, group_bias, norm_gain
):
    pixel_count = pixels.shape[2]
    choose, to_group = slot_tables(group_map)
    source_pixels = lax.all_to_all(pixels, "chan", split_axis=0, concat_axis=1, tiled=True)
    source_mask = lax.all_to_all(patch_mask, "chan", split_axis=0, concat_axis=1, tiled=True)
    offsets = gathered(chan_embed, "chan", 0).astype(F32)
    weights = gathered(agg_weight, "chan", 0)
    section = gathered(embed_weight, "loc", 1)
    rows, channels, _ = source_pixels.shape
    features = section.shape[1]
    projected = jnp.dot(source_pixels.reshape(rows * channels, pixel_count), section, preferred_element_type=F32)
    projected = projected.reshape(rows, channels, features)
    hidden = source_mask.reshape(rows, channels, 1) == 1
    pre = jnp.where(hidden, mask_token.astype(F32)[None, None, :], projected) + offsets[None]
    weighted = (jax.nn.gelu(pre, approximate=False) * weights[None, :, None]).astype(BF16)
    bundled = weighted.reshape(rows, channels // BUNDLE, BUNDLE, features)
    sums = jnp.einsum("lbke,bsk->lbse", bundled, choose, preferred_element_type=F32)
    sums = sums.reshape(rows, channels // BUNDLE * 2, features).astype(BF16)
    aggregate = jnp.einsum("gq,lqe->lge", to_group, sums, preferred_element_type=F32)
    return attend(aggregate, query_key, group_bias, norm_gain)


def plain_shards(
    pixels,
    patch_mask,
    group_map,
    embed_weight,
    mask_token,
    chan_embed,
    agg_weight,
    query_key,
    group_bias,
    norm_gain,
    head_weight,
    head_bias,
):
    _, own_channels, pixel_count = pixels.shape
    joined = plain_join(
        pixels, patch_mask, group_map, embed_weight, mask_token, chan_embed, agg_weight, query_key, group_bias, norm_gain
    )
    section = gathered(joined, "chan", 0)
    flat_heads = head_weight.reshape(-1, own_channels * pixel_count)
    decoded = jnp.dot(section, flat_heads, preferred_element_type=F32) + head_bias.reshape(1, -1)
    return decoded.astype(BF16).reshape(section.shape[0], own_channels, pixel_count)


def pack_kernel(rows, pixels_ref, mask_ref, weight_ref, out_ref):
    peers, pair_rows, width = pixels_ref.shape
    own, locations = mask_ref.shape
    per = locations // peers
    spread = (iota((own, pair_rows), 1) % own == iota((own, pair_rows), 0)).astype(BF16)
    by_location = dot(mask_ref[...].astype(F32).astype(BF16), spread, 0, 0)
    by_location = by_location.reshape(peers, per, pair_rows)
    keep = iota((1, per, pair_rows), 2) // own == iota((1, per, pair_rows), 1)
    hidden = jnp.sum(jnp.where(keep, by_location, 0.0), axis=1)
    visible = 1.0 - hidden
    before = (iota((pair_rows, pair_rows), 0) < iota((pair_rows, pair_rows), 1)).astype(BF16)
    rank = dot(visible.astype(BF16), before)
    place = jnp.where(visible > 0.5, rank, -1.0)
    limit = float(rows - 2)
    over = jnp.max(place, keepdims=True) >= limit
    marked = hidden + jnp.where(over, 2.0, 0.0)
    weight = weight_ref[...]
    high = weight.astype(BF16)
    middle = (weight - high.astype(F32)).astype(BF16)
    low = (weight - high.astype(F32) - middle.astype(F32)).astype(BF16)
    lane = iota((own, width), 1)
    line = iota((own, width), 0)
    weight_row = jnp.zeros((1, width), F32)
    for part, value in enumerate((high, middle, low)):
        weight_row += dot(value, (lane == line + part * own).astype(BF16))
    index = iota((rows, pair_rows), 0).astype(F32)
    for peer in range(peers):
        chosen = (place[peer : peer + 1, :] == index).astype(BF16)
        packed = dot(chosen, pixels_ref[peer])
        line = iota((rows, width), 0)
        mask_row = jnp.pad(marked[peer : peer + 1, :], ((0, 0), (0, width - pair_rows)))
        packed = jnp.where(line == rows - 2, weight_row, packed)
        packed = jnp.where(line == rows - 1, mask_row, packed)
        out_ref[peer] = packed.astype(BF16)


def by_channel_kernel(start, head_ref, out_ref, blocks, arrived):
    _, depth, own, width = blocks.shape
    steps = out_ref.shape[1] // depth

    def fetch(step):
        slot = step % 2
        rows = pl.ds(start + step * depth, depth)
        return pltpu.make_async_copy(head_ref.at[rows], blocks.at[slot], arrived.at[slot])

    fetch(0).start()
    for step in range(steps):
        if step + 1 < steps:
            fetch(step + 1).start()
        fetch(step).wait()
        out_ref[:, step * depth : (step + 1) * depth, :] = jnp.swapaxes(blocks[step % 2], 0, 1)


def join_kernel(
    sizes,
    place_ref,
    packed_ref,
    *refs,
):
    sources, own, per, heads, chunk = sizes
    section_refs = refs[: sizes_sections(refs)]
    rest = refs[len(section_refs) :]
    (chan_ref, other_ref, token_ref, query_ref, group_ref, bias_ref, gain_ref, out_ref, over_ref) = rest[:9]
    (embed, offset, table, choice, where, value, score) = rest[9:]
    _, rows, width = packed_ref.shape
    total = sources * rows
    features = embed.shape[1]
    channels = sources * own
    pair_rows = per * own
    depth = features // heads
    chunks = total // chunk

    me_loc = place_ref[0]
    me = place_ref[1]
    sections = len(section_refs)
    part = features // sections
    for step, section in enumerate(section_refs):
        at = lax.rem(me_loc + step, sections) * part
        embed[:, pl.ds(pl.multiple_of(at, part), part)] = section[...]
    half = sources // 2
    for step in range(half):
        for ref, flip in ((chan_ref, 0), (other_ref, 1)):
            source = jnp.bitwise_xor(me, 2 * step + flip)
            offset[pl.ds(pl.multiple_of(source * own, own), own), :] = ref[step * own : (step + 1) * own, :]

    last = [packed_ref[s, rows - 16 :, :].astype(F32) for s in range(sources)]
    marked = jnp.concatenate([tail[15:16, :] for tail in last], axis=0)[:, :pair_rows]
    weight_rows = jnp.concatenate([tail[14:15, :] for tail in last], axis=0)
    over = jnp.max((marked >= 2.0).astype(F32), keepdims=True)
    over_ref[...] = jnp.broadcast_to(over, over_ref.shape).astype(jnp.int32)
    hidden = jnp.where(marked >= 2.0, marked - 2.0, marked)
    visible = 1.0 - hidden
    before = (iota((pair_rows, pair_rows), 0) < iota((pair_rows, pair_rows), 1)).astype(BF16)
    rank = dot(visible.astype(BF16), before)
    place = jnp.where(visible > 0.5, rank, -1.0)
    index = iota((rows, pair_rows), 0).astype(F32)
    of_row = iota((pair_rows, LANES), 0) // own
    to_location = (of_row == iota((pair_rows, LANES), 1)).astype(BF16)
    channel_of_row = iota((pair_rows, channels), 0) % own
    for s in range(sources):
        chosen = (place[s : s + 1, :] == index).astype(BF16)
        to_channel = (channel_of_row + s * own == iota((pair_rows, channels), 1)).astype(BF16)
        choice[s * rows : (s + 1) * rows, :] = dot(chosen, to_channel).astype(BF16)
        where[s * rows : (s + 1) * rows, :] = dot(chosen, to_location).astype(BF16)
    lane = iota((width, channels), 0)
    spread = ((lane % own == iota((width, channels), 1) % own) & (lane < 3 * own)).astype(BF16)
    each = dot(weight_rows.astype(BF16), spread)
    mine = iota((sources, channels), 1) // own == iota((sources, channels), 0)
    weight = jnp.sum(jnp.where(mine, each, 0.0), axis=0, keepdims=True)

    block = 256
    for at in range(0, features, block):
        cols = slice(at, at + block)
        table[:, cols] = gelu(token_ref[:, cols].astype(F32) + offset[:, cols].astype(F32)).astype(BF16)
    table_score = dot(query_ref[...], table[...], 1, 1)

    eye = (iota((per, LANES), 0) == iota((per, LANES), 1)).astype(BF16)
    tile = 128
    counts = jnp.zeros((per, channels), F32)
    spread_score = jnp.zeros((heads * per, channels), F32)
    for c in range(chunks):
        base = c * chunk
        for at in range(0, features, block):
            cols = slice(at, at + block)
            for top in range(base, base + chunk, tile):
                line = slice(top, top + tile)
                pixel = packed_ref[...].reshape(total, width)[line, :]
                pre = dot(pixel, embed[:, cols]) + dot(choice[line, :], offset[:, cols])
                value[line, cols] = gelu(pre).astype(BF16)
        line = slice(base, base + chunk)
        score[c] = dot(query_ref[...], value[line, :], 1, 1)
        at_location = dot(eye, where[line, :], 1, 1)
        counts += dot(at_location.astype(BF16), choice[line, :])
        by_row = [score[c, h : h + 1, :] * at_location for h in range(heads)]
        for piece in halves(jnp.concatenate(by_row, axis=0)):
            spread_score += dot(piece, choice[line, :])

    hidden_at = 1.0 - counts
    by_row = [hidden_at * table_score[h : h + 1, :] for h in range(heads)]
    full = (spread_score + jnp.concatenate(by_row, axis=0)) * weight
    groups = bias_ref.shape[1]
    to_group = (iota((groups, channels), 0) == group_ref[...]).astype(BF16)
    scores = sum(dot(piece, to_group, 1, 1) for piece in halves(full))
    scores += jnp.concatenate([jnp.broadcast_to(bias_ref[h : h + 1, :], (per, groups)) for h in range(heads)], axis=0)
    scores = jnp.exp(scores - jnp.max(scores, axis=-1, keepdims=True))
    attention = scores / jnp.sum(scores, axis=-1, keepdims=True)
    each = sum(dot(piece, to_group) for piece in halves(attention)) * weight

    of_table = halves(each * jnp.concatenate([hidden_at] * heads, axis=0))
    each = halves(each)
    pooled = [jnp.zeros((2 * per, depth), F32)] * heads

    def stack(pieces, h):
        return jnp.concatenate([piece[h * per : (h + 1) * per, :] for piece in pieces], axis=0)

    for h in range(heads):
        pooled[h] += dot(stack(of_table, h), table[:, h * depth : (h + 1) * depth])
    for c in range(chunks):
        line = slice(c * chunk, (c + 1) * chunk)
        at_location = dot(eye, where[line, :], 1, 1)
        spread_each = sum(dot(piece, choice[line, :], 1, 1) for piece in each)
        pieces = halves(spread_each * jnp.concatenate([at_location] * heads, axis=0))
        for h in range(heads):
            pooled[h] += dot(stack(pieces, h), value[line, h * depth : (h + 1) * depth])
    pooled = [both[:per] + both[per:] for both in pooled]
    square = sum(jnp.sum(rows_of * rows_of, axis=-1, keepdims=True) for rows_of in pooled)
    scale = lax.rsqrt(square * (1.0 / features) + 1e-06)
    for h in range(heads):
        cols = slice(h * depth, (h + 1) * depth)
        out_ref[:, cols] = (pooled[h] * scale * gain_ref[:, cols]).astype(BF16)


def sizes_sections(refs):
    return len(refs) - 16


def decode_kernel(place_ref, near_ref, far_ref, low_ref, high_ref, bias_ref, *refs):
    *most, out_ref, over_ref, joined, decoded = refs
    own = bias_ref.shape[0]
    over_ref[0] = jnp.max(functools.reduce(jnp.maximum, [ref[...] for ref in most]))
    half = near_ref.shape[0]
    per = out_ref.shape[1]
    me = place_ref[1]
    split = low_ref.shape[1]
    joined[:half] = near_ref[...]
    joined[half:] = far_ref[...]
    for c in range(own):
        value = dot(joined[:, :split], low_ref[c]) + dot(joined[:, split:], high_ref[c])
        decoded[c] = (value + bias_ref[c : c + 1, :]).astype(BF16)
    for flip in range(2):
        for step in range(half // per):
            owner = jnp.bitwise_xor(me, 2 * step + flip)
            top = flip * half + step * per
            out_ref[owner] = jnp.swapaxes(decoded[:, top : top + per, :], 0, 1)


def flipped(value, axis, count, flip):
    return lax.ppermute(value, axis, [(i, i ^ flip) for i in range(count)])


def spread_rows(value, axis, count):
    across = flipped(value, axis, count, count // 2)
    near = []
    for rows in (value, across):
        near += [rows] + [flipped(rows, axis, count, 2 * k) for k in range(1, count // 4)]
    near = jnp.concatenate(near, axis=0)
    return near, flipped(near, axis, count, 1)


def shards(
    peers,
    blocks,
    pixels,
    patch_mask,
    group_map,
    embed_weight,
    mask_token,
    chan_embed,
    agg_weight,
    query_key,
    group_bias,
    norm_gain,
    head_weight,
    head_bias,
):
    locations, own, pixel_count = pixels.shape
    channels = group_map.shape[0]
    heads, features = query_key.shape
    per = locations // peers
    pair_rows = per * own
    rows = -(-pair_rows * 3 // 8 // 16) * 16
    total = peers * rows
    fits = (
        peers & (peers - 1) == 0
        and own % 16 == 0
        and per % 16 == 0
        and pair_rows <= pixel_count
        and 3 * own <= pixel_count
        and total % 512 == 0
    )
    if not fits:
        return plain_shards(
            pixels,
            patch_mask,
            group_map,
            embed_weight,
            mask_token,
            chan_embed,
            agg_weight,
            query_key,
            group_bias,
            norm_gain,
            head_weight,
            head_bias,
        )
    vmem = pltpu.CompilerParams(vmem_limit_bytes=24 << 20)
    place = jnp.stack([lax.axis_index("loc"), lax.axis_index("chan")]).astype(jnp.int32)

    packed = pl.pallas_call(
        functools.partial(pack_kernel, rows),
        out_shape=jax.ShapeDtypeStruct((peers, rows, pixel_count), BF16),
        in_specs=[VMEM] * 3,
        out_specs=VMEM,
        compiler_params=vmem,
        name="pack",
    )(pixels.reshape(peers, pair_rows, pixel_count), patch_mask.T, agg_weight.reshape(1, own))
    packed, sent_weight, sent_embed = lax.optimization_barrier((packed, embed_weight, chan_embed))
    packed = lax.all_to_all(packed, "chan", split_axis=0, concat_axis=0, tiled=True)
    sections = [embed_weight]
    for step in range(1, blocks):
        hop = [(i, (i - step) % blocks) for i in range(blocks)]
        sections.append(lax.ppermute(sent_weight, "loc", hop))
    near, far = spread_rows(sent_embed, "chan", peers)
    chunk = 512
    joined, over = pl.pallas_call(
        functools.partial(join_kernel, (peers, own, per, heads, chunk)),
        out_shape=(
            jax.ShapeDtypeStruct((per, features), BF16),
            jax.ShapeDtypeStruct((8, LANES), jnp.int32),
        ),
        in_specs=[SMEM] + [VMEM] * (8 + blocks),
        out_specs=(VMEM, VMEM),
        scratch_shapes=[
            pltpu.VMEM((pixel_count, features), BF16),
            pltpu.VMEM((channels, features), BF16),
            pltpu.VMEM((channels, features), BF16),
            pltpu.VMEM((total, channels), BF16),
            pltpu.VMEM((total, LANES), BF16),
            pltpu.VMEM((total, features), BF16),
            pltpu.VMEM((total // chunk, heads, chunk), F32),
        ],
        compiler_params=vmem,
        name="join",
    )(
        place,
        packed,
        *sections,
        near,
        far,
        mask_token.reshape(1, features),
        query_key,
        group_map.reshape(1, channels),
        group_bias,
        norm_gain.reshape(1, features),
    )
    most = [over]
    for step in range(1, blocks):
        hop = [(i, (i - step) % blocks) for i in range(blocks)]
        most.append(lax.ppermute(over, "loc", hop))
    split = features // 2

    def by_channel(start):
        block = 256
        return pl.pallas_call(
            functools.partial(by_channel_kernel, start),
            out_shape=jax.ShapeDtypeStruct((own, split, pixel_count), BF16),
            in_specs=[ANY],
            out_specs=VMEM,
            scratch_shapes=[
                pltpu.VMEM((2, block, own, pixel_count), BF16),
                pltpu.SemaphoreType.DMA((2,)),
            ],
            compiler_params=vmem,
            cost_estimate=pl.CostEstimate(flops=0, bytes_accessed=4 * own * split * pixel_count, transcendentals=0),
            name="by_channel",
        )(sent_head)

    joined, sent_head = lax.optimization_barrier((joined, head_weight))
    parts = [by_channel(start) for start in range(0, features, split)]
    near, far = spread_rows(joined, "chan", peers)
    rebuilt, over = pl.pallas_call(
        decode_kernel,
        out_shape=(
            jax.ShapeDtypeStruct((peers, per, own, pixel_count), BF16),
            jax.ShapeDtypeStruct((1,), jnp.int32),
        ),
        in_specs=[SMEM] + [VMEM] * (5 + blocks),
        out_specs=(VMEM, SMEM),
        scratch_shapes=[
            pltpu.VMEM((locations, features), BF16),
            pltpu.VMEM((own, locations, pixel_count), BF16),
        ],
        compiler_params=vmem,
        name="decode",
    )(place, near, far, *parts, head_bias, *most)
    return lax.cond(
        over[0] > 0,
        lambda: plain_shards(
            pixels,
            patch_mask,
            group_map,
            embed_weight,
            mask_token,
            chan_embed,
            agg_weight,
            query_key,
            group_bias,
            norm_gain,
            head_weight,
            head_bias,
        ),
        lambda: rebuilt.reshape(locations, own, pixel_count),
    )


def solution(mesh):
    return jax.shard_map(
        functools.partial(shards, mesh.shape["chan"], mesh.shape["loc"]),
        mesh=mesh,
        in_specs=(
            P("loc", "chan", None),
            P("loc", "chan"),
            P(),
            P(None, "loc"),
            P(),
            P("chan", None),
            P("chan"),
            P(),
            P(),
            P(),
            P(None, "chan", None),
            P("chan", None),
        ),
        out_specs=P("loc", "chan", None),
        check_vma=False,
    )
```

```python
import functools

import jax
import jax.numpy as jnp
from jax import lax
from jax.experimental import pallas as pl
from jax.experimental.pallas import tpu as pltpu
from jax.sharding import PartitionSpec as P

G = 64
BUNDLE = 4
LANES = 128
VMEM = pl.BlockSpec(memory_space=pltpu.VMEM)
SMEM = pl.BlockSpec(memory_space=pltpu.SMEM)
HBM = pl.BlockSpec(memory_space=pltpu.HBM)
ANY = pl.BlockSpec(memory_space=pl.ANY)
F32, BF16 = jnp.float32, jnp.bfloat16


def dot(left, right, left_dim=1, right_dim=0):
    dims = (((left_dim,), (right_dim,)), ((), ()))
    return lax.dot_general(left, right, dims, preferred_element_type=F32)


def iota(shape, axis):
    return lax.broadcasted_iota(jnp.int32, shape, axis)


def halves(value):
    high = value.astype(BF16)
    return high, (value - high.astype(F32)).astype(BF16)


def gelu(value):
    return 0.5 * value * (1.0 + lax.erf(value * 0.7071067811865476))


def slot_tables(group_map):
    bundled = group_map.reshape(-1, BUNDLE)
    lowest = jnp.min(bundled, axis=1)
    highest = jnp.max(bundled, axis=1)
    slot_index = (bundled != lowest[:, None]).astype(jnp.int32)
    choose = slot_index[:, None, :] == jnp.arange(2, dtype=jnp.int32)[None, :, None]
    slot_group = jnp.stack([lowest, highest], axis=1).reshape(-1)
    to_group = jnp.arange(G, dtype=jnp.int32)[:, None] == slot_group[None, :]
    return (choose.astype(BF16), to_group.astype(BF16))


def attend(aggregate, query_key, group_bias, norm_gain):
    rows, _, features = aggregate.shape
    heads = query_key.shape[0]
    high = lax.Precision.HIGHEST
    scores = jnp.einsum("lge,he->lhg", aggregate, query_key.astype(F32), precision=high)
    weights = jax.nn.softmax(scores + group_bias[None], axis=-1)
    split = aggregate.reshape(rows, G, heads, features // heads)
    pooled = jnp.einsum("lhg,lghd->lhd", weights, split, precision=high).reshape(rows, features)
    inverse_rms = lax.rsqrt(jnp.mean(pooled * pooled, axis=-1, keepdims=True) + 1e-06)
    return (pooled * inverse_rms * norm_gain[None]).astype(BF16)


def gathered(value, axis, dim):
    count = lax.axis_size(axis)
    copies = jnp.broadcast_to(value[None], (count,) + value.shape)
    parts = lax.all_to_all(copies, axis, split_axis=0, concat_axis=0, tiled=True)
    parts = jnp.moveaxis(parts, 0, dim)
    return parts.reshape(value.shape[:dim] + (-1,) + value.shape[dim + 1 :])


def plain_join(
    pixels, patch_mask, group_map, embed_weight, mask_token, chan_embed, agg_weight, query_key, group_bias, norm_gain
):
    pixel_count = pixels.shape[2]
    choose, to_group = slot_tables(group_map)
    source_pixels = lax.all_to_all(pixels, "chan", split_axis=0, concat_axis=1, tiled=True)
    source_mask = lax.all_to_all(patch_mask, "chan", split_axis=0, concat_axis=1, tiled=True)
    offsets = gathered(chan_embed, "chan", 0).astype(F32)
    weights = gathered(agg_weight, "chan", 0)
    section = gathered(embed_weight, "loc", 1)
    rows, channels, _ = source_pixels.shape
    features = section.shape[1]
    projected = jnp.dot(source_pixels.reshape(rows * channels, pixel_count), section, preferred_element_type=F32)
    projected = projected.reshape(rows, channels, features)
    hidden = source_mask.reshape(rows, channels, 1) == 1
    pre = jnp.where(hidden, mask_token.astype(F32)[None, None, :], projected) + offsets[None]
    weighted = (jax.nn.gelu(pre, approximate=False) * weights[None, :, None]).astype(BF16)
    bundled = weighted.reshape(rows, channels // BUNDLE, BUNDLE, features)
    sums = jnp.einsum("lbke,bsk->lbse", bundled, choose, preferred_element_type=F32)
    sums = sums.reshape(rows, channels // BUNDLE * 2, features).astype(BF16)
    aggregate = jnp.einsum("gq,lqe->lge", to_group, sums, preferred_element_type=F32)
    return attend(aggregate, query_key, group_bias, norm_gain)


def plain_shards(
    pixels,
    patch_mask,
    group_map,
    embed_weight,
    mask_token,
    chan_embed,
    agg_weight,
    query_key,
    group_bias,
    norm_gain,
    head_weight,
    head_bias,
):
    _, own_channels, pixel_count = pixels.shape
    joined = plain_join(
        pixels, patch_mask, group_map, embed_weight, mask_token, chan_embed, agg_weight, query_key, group_bias, norm_gain
    )
    section = gathered(joined, "chan", 0)
    flat_heads = head_weight.reshape(-1, own_channels * pixel_count)
    decoded = jnp.dot(section, flat_heads, preferred_element_type=F32) + head_bias.reshape(1, -1)
    return decoded.astype(BF16).reshape(section.shape[0], own_channels, pixel_count)


def near_flip(block, count):
    quarter = count // 4
    return block // quarter * (count // 2) + (block + 1) % quarter * 2


def pack_kernel(rows, pixels_ref, mask_ref, weight_ref, out_ref):
    peers, pair_rows, width = pixels_ref.shape
    own, locations = mask_ref.shape
    per = locations // peers
    spread = (iota((own, pair_rows), 1) % own == iota((own, pair_rows), 0)).astype(BF16)
    by_location = dot(mask_ref[...].astype(F32).astype(BF16), spread, 0, 0)
    by_location = by_location.reshape(peers, per, pair_rows)
    keep = iota((1, per, pair_rows), 2) // own == iota((1, per, pair_rows), 1)
    hidden = jnp.sum(jnp.where(keep, by_location, 0.0), axis=1)
    visible = 1.0 - hidden
    before = (iota((pair_rows, pair_rows), 0) < iota((pair_rows, pair_rows), 1)).astype(BF16)
    rank = dot(visible.astype(BF16), before)
    place = jnp.where(visible > 0.5, rank, -1.0)
    limit = float(rows - 2)
    over = jnp.max(place, keepdims=True) >= limit
    marked = hidden + jnp.where(over, 2.0, 0.0)
    weight = weight_ref[...]
    high = weight.astype(BF16)
    middle = (weight - high.astype(F32)).astype(BF16)
    low = (weight - high.astype(F32) - middle.astype(F32)).astype(BF16)
    lane = iota((own, width), 1)
    line = iota((own, width), 0)
    weight_row = jnp.zeros((1, width), F32)
    for part, value in enumerate((high, middle, low)):
        weight_row += dot(value, (lane == line + part * own).astype(BF16))
    index = iota((rows, pair_rows), 0).astype(F32)
    for peer in range(peers):
        chosen = (place[peer : peer + 1, :] == index).astype(BF16)
        packed = dot(chosen, pixels_ref[peer])
        line = iota((rows, width), 0)
        mask_row = jnp.pad(marked[peer : peer + 1, :], ((0, 0), (0, width - pair_rows)))
        packed = jnp.where(line == rows - 2, weight_row, packed)
        packed = jnp.where(line == rows - 1, mask_row, packed)
        out_ref[peer] = packed.astype(BF16)


def fetched_rows(start, steps, head_ref, blocks, arrived):
    depth = blocks.shape[1]

    def fetch(step):
        rows = pl.ds(start + step * depth, depth)
        return pltpu.make_async_copy(head_ref.at[rows], blocks.at[step % 2], arrived.at[step % 2])

    fetch(0).start()
    for step in range(steps):
        if step + 1 < steps:
            fetch(step + 1).start()
        fetch(step).wait()
        yield step, blocks[step % 2]


def early_heads_kernel(start, head_ref, out_ref, blocks, turned, arrived, left):
    depth = blocks.shape[1]
    steps = out_ref.shape[1] // depth

    def store(step):
        rows = pl.ds(step * depth, depth)
        return pltpu.make_async_copy(turned.at[step % 2], out_ref.at[:, rows, :], left.at[step % 2])

    for step, rows in fetched_rows(start, steps, head_ref, blocks, arrived):
        if step >= 2:
            store(step - 2).wait()
        turned[step % 2] = jnp.swapaxes(rows, 0, 1)
        store(step).start()
    for step in range(max(steps - 2, 0), steps):
        store(step).wait()


def late_heads_kernel(start, across_ref, head_ref, *refs):
    *most, out_ref, again_ref, over_ref, blocks, arrived = refs
    over_ref[0] = jnp.max(functools.reduce(jnp.maximum, [ref[...] for ref in most]))
    depth = blocks.shape[1]
    again_ref[...] = across_ref[...]
    for step, rows in fetched_rows(start, out_ref.shape[1] // depth, head_ref, blocks, arrived):
        out_ref[:, step * depth : (step + 1) * depth, :] = jnp.swapaxes(rows, 0, 1)


def join_kernel(
    sizes,
    place_ref,
    packed_ref,
    *refs,
):
    sources, own, per, heads, chunk = sizes
    section_refs = refs[: sizes_sections(refs)]
    rest = refs[len(section_refs) :]
    (chan_ref, other_ref, token_ref, query_ref, group_ref, bias_ref, gain_ref, out_ref, over_ref) = rest[:9]
    (embed, offset, table, choice, where, value, score) = rest[9:]
    _, rows, width = packed_ref.shape
    total = sources * rows
    features = embed.shape[1]
    channels = sources * own
    pair_rows = per * own
    depth = features // heads
    chunks = total // chunk

    me_loc = place_ref[0]
    me = place_ref[1]
    sections = len(section_refs)
    part = features // sections
    for step, section in enumerate(section_refs):
        at = lax.rem(me_loc + step, sections) * part
        embed[:, pl.ds(pl.multiple_of(at, part), part)] = section[...]
    half = sources // 2
    for step in range(half):
        for ref, flip in ((chan_ref, 0), (other_ref, 1)):
            source = jnp.bitwise_xor(me, near_flip(step, sources) + flip)
            offset[pl.ds(pl.multiple_of(source * own, own), own), :] = ref[step * own : (step + 1) * own, :]

    last = [packed_ref[s, rows - 16 :, :].astype(F32) for s in range(sources)]
    marked = jnp.concatenate([tail[15:16, :] for tail in last], axis=0)[:, :pair_rows]
    weight_rows = jnp.concatenate([tail[14:15, :] for tail in last], axis=0)
    over = jnp.max((marked >= 2.0).astype(F32), keepdims=True)
    over_ref[...] = jnp.broadcast_to(over, over_ref.shape).astype(jnp.int32)
    hidden = jnp.where(marked >= 2.0, marked - 2.0, marked)
    visible = 1.0 - hidden
    before = (iota((pair_rows, pair_rows), 0) < iota((pair_rows, pair_rows), 1)).astype(BF16)
    rank = dot(visible.astype(BF16), before)
    place = jnp.where(visible > 0.5, rank, -1.0)
    index = iota((rows, pair_rows), 0).astype(F32)
    of_row = iota((pair_rows, LANES), 0) // own
    to_location = (of_row == iota((pair_rows, LANES), 1)).astype(BF16)
    channel_of_row = iota((pair_rows, channels), 0) % own
    for s in range(sources):
        chosen = (place[s : s + 1, :] == index).astype(BF16)
        to_channel = (channel_of_row + s * own == iota((pair_rows, channels), 1)).astype(BF16)
        choice[s * rows : (s + 1) * rows, :] = dot(chosen, to_channel).astype(BF16)
        where[s * rows : (s + 1) * rows, :] = dot(chosen, to_location).astype(BF16)
    lane = iota((width, channels), 0)
    spread = ((lane % own == iota((width, channels), 1) % own) & (lane < 3 * own)).astype(BF16)
    each = dot(weight_rows.astype(BF16), spread)
    mine = iota((sources, channels), 1) // own == iota((sources, channels), 0)
    weight = jnp.sum(jnp.where(mine, each, 0.0), axis=0, keepdims=True)

    block = 256
    for at in range(0, features, block):
        cols = slice(at, at + block)
        table[:, cols] = gelu(token_ref[:, cols].astype(F32) + offset[:, cols].astype(F32)).astype(BF16)
    table_score = dot(query_ref[...], table[...], 1, 1)

    eye = (iota((per, LANES), 0) == iota((per, LANES), 1)).astype(BF16)
    tile = chunk
    counts = jnp.zeros((per, channels), F32)
    spread_score = jnp.zeros((heads * per, channels), F32)
    for c in range(chunks):
        base = c * chunk
        for at in range(0, features, block):
            cols = slice(at, at + block)
            for top in range(base, base + chunk, tile):
                line = slice(top, top + tile)
                pixel = packed_ref[...].reshape(total, width)[line, :]
                pre = dot(pixel, embed[:, cols]) + dot(choice[line, :], offset[:, cols])
                value[line, cols] = gelu(pre).astype(BF16)
        line = slice(base, base + chunk)
        score[c] = dot(query_ref[...], value[line, :], 1, 1)
        at_location = dot(eye, where[line, :], 1, 1)
        counts += dot(at_location.astype(BF16), choice[line, :])
        by_row = [score[c, h : h + 1, :] * at_location for h in range(heads)]
        for piece in halves(jnp.concatenate(by_row, axis=0)):
            spread_score += dot(piece, choice[line, :])

    hidden_at = 1.0 - counts
    by_row = [hidden_at * table_score[h : h + 1, :] for h in range(heads)]
    full = (spread_score + jnp.concatenate(by_row, axis=0)) * weight
    groups = bias_ref.shape[1]
    to_group = (iota((groups, channels), 0) == group_ref[...]).astype(BF16)
    scores = sum(dot(piece, to_group, 1, 1) for piece in halves(full))
    scores += jnp.concatenate([jnp.broadcast_to(bias_ref[h : h + 1, :], (per, groups)) for h in range(heads)], axis=0)
    scores = jnp.exp(scores - jnp.max(scores, axis=-1, keepdims=True))
    attention = scores / jnp.sum(scores, axis=-1, keepdims=True)
    each = sum(dot(piece, to_group) for piece in halves(attention)) * weight

    of_table = halves(each * jnp.concatenate([hidden_at] * heads, axis=0))
    each = halves(each)
    pooled = [jnp.zeros((2 * per, depth), F32)] * heads

    def stack(pieces, h):
        return jnp.concatenate([piece[h * per : (h + 1) * per, :] for piece in pieces], axis=0)

    for h in range(heads):
        pooled[h] += dot(stack(of_table, h), table[:, h * depth : (h + 1) * depth])
    for c in range(chunks):
        line = slice(c * chunk, (c + 1) * chunk)
        at_location = dot(eye, where[line, :], 1, 1)
        spread_each = sum(dot(piece, choice[line, :], 1, 1) for piece in each)
        pieces = halves(spread_each * jnp.concatenate([at_location] * heads, axis=0))
        for h in range(heads):
            pooled[h] += dot(stack(pieces, h), value[line, h * depth : (h + 1) * depth])
    pooled = [both[:per] + both[per:] for both in pooled]
    square = sum(jnp.sum(rows_of * rows_of, axis=-1, keepdims=True) for rows_of in pooled)
    scale = lax.rsqrt(square * (1.0 / features) + 1e-06)
    for h in range(heads):
        cols = slice(h * depth, (h + 1) * depth)
        out_ref[:, cols] = (pooled[h] * scale * gain_ref[:, cols]).astype(BF16)


def sizes_sections(refs):
    return len(refs) - 16


def decode_kernel(place_ref, near_ref, far_ref, low_ref, high_ref, bias_ref, out_ref, joined, decoded):
    own = bias_ref.shape[0]
    half = near_ref.shape[0]
    count, per = out_ref.shape[:2]
    me = place_ref[1]
    split = low_ref.shape[1]
    joined[:half] = near_ref[...]
    joined[half:] = far_ref[...]
    for c in range(own):
        value = dot(joined[:, :split], low_ref[c]) + dot(joined[:, split:], high_ref[c])
        decoded[c] = (value + bias_ref[c : c + 1, :]).astype(BF16)
    for flip in range(2):
        for step in range(half // per):
            owner = jnp.bitwise_xor(me, near_flip(step, count) + flip)
            top = flip * half + step * per
            out_ref[owner] = jnp.swapaxes(decoded[:, top : top + per, :], 0, 1)


def flipped(value, axis, count, flip):
    return lax.ppermute(value, axis, [(i, i ^ flip) for i in range(count)])


def near_rows(value, across, axis, count, again=None):
    near = []
    for rows, own in ((value, value), (across, across if again is None else again)):
        near += [flipped(rows, axis, count, 2 * k) for k in range(1, count // 4)] + [own]
    return jnp.concatenate(near, axis=0)


def shards(
    peers,
    blocks,
    pixels,
    patch_mask,
    group_map,
    embed_weight,
    mask_token,
    chan_embed,
    agg_weight,
    query_key,
    group_bias,
    norm_gain,
    head_weight,
    head_bias,
):
    locations, own, pixel_count = pixels.shape
    channels = group_map.shape[0]
    heads, features = query_key.shape
    per = locations // peers
    pair_rows = per * own
    rows = -(-pair_rows * 3 // 8 // 16) * 16
    total = peers * rows
    fits = (
        peers & (peers - 1) == 0
        and own % 16 == 0
        and per % 16 == 0
        and pair_rows <= pixel_count
        and 3 * own <= pixel_count
        and total % 512 == 0
    )
    if not fits:
        return plain_shards(
            pixels,
            patch_mask,
            group_map,
            embed_weight,
            mask_token,
            chan_embed,
            agg_weight,
            query_key,
            group_bias,
            norm_gain,
            head_weight,
            head_bias,
        )
    vmem = pltpu.CompilerParams(vmem_limit_bytes=24 << 20)
    place = jnp.stack([lax.axis_index("loc"), lax.axis_index("chan")]).astype(jnp.int32)

    packed = pl.pallas_call(
        functools.partial(pack_kernel, rows),
        out_shape=jax.ShapeDtypeStruct((peers, rows, pixel_count), BF16),
        in_specs=[VMEM] * 3,
        out_specs=VMEM,
        compiler_params=vmem,
        name="pack",
    )(pixels.reshape(peers, pair_rows, pixel_count), patch_mask.T, agg_weight.reshape(1, own))
    packed, sent_weight, sent_embed = lax.optimization_barrier((packed, embed_weight, chan_embed))
    packed = lax.all_to_all(packed, "chan", split_axis=0, concat_axis=0, tiled=True)
    sections = [embed_weight]
    for step in range(1, blocks):
        hop = [(i, (i - step) % blocks) for i in range(blocks)]
        sections.append(lax.ppermute(sent_weight, "loc", hop))
    split = features // 2
    block = 256
    turned = [pltpu.VMEM((2, block, own, pixel_count), BF16), pltpu.VMEM((2, own, block, pixel_count), BF16)]
    landed = [pltpu.SemaphoreType.DMA((2,))] * 2
    turn_cost = pl.CostEstimate(flops=0, bytes_accessed=4 * own * split * pixel_count, transcendentals=0)
    across = flipped(sent_embed, "chan", peers, peers // 2)
    across, sent_head = lax.optimization_barrier((across, head_weight))
    early = pl.pallas_call(
        functools.partial(early_heads_kernel, 0),
        out_shape=pltpu.HBM((own, split, pixel_count), BF16),
        in_specs=[ANY],
        out_specs=HBM,
        scratch_shapes=turned + landed,
        compiler_params=vmem,
        cost_estimate=turn_cost,
        name="early_heads",
    )(sent_head)
    near = near_rows(sent_embed, across, "chan", peers)
    near, early = lax.optimization_barrier((near, early))
    far = flipped(near, "chan", peers, 1)
    chunk = 512
    joined, over = pl.pallas_call(
        functools.partial(join_kernel, (peers, own, per, heads, chunk)),
        out_shape=(
            jax.ShapeDtypeStruct((per, features), BF16),
            jax.ShapeDtypeStruct((8, LANES), jnp.int32),
        ),
        in_specs=[SMEM] + [VMEM] * (8 + blocks),
        out_specs=(VMEM, VMEM),
        scratch_shapes=[
            pltpu.VMEM((pixel_count, features), BF16),
            pltpu.VMEM((channels, features), BF16),
            pltpu.VMEM((channels, features), BF16),
            pltpu.VMEM((total, channels), BF16),
            pltpu.VMEM((total, LANES), BF16),
            pltpu.VMEM((total, features), BF16),
            pltpu.VMEM((total // chunk, heads, chunk), F32),
        ],
        compiler_params=vmem,
        cost_estimate=pl.CostEstimate(
            flops=4 * total * features * (pixel_count + 3 * channels),
            bytes_accessed=2 * features * (pixel_count + channels),
            transcendentals=0,
        ),
        name="join",
    )(
        place,
        packed,
        *sections,
        near,
        far,
        mask_token.reshape(1, features),
        query_key,
        group_map.reshape(1, channels),
        group_bias,
        norm_gain.reshape(1, features),
    )
    most = [over]
    for step in range(1, blocks):
        hop = [(i, (i - step) % blocks) for i in range(blocks)]
        most.append(lax.ppermute(over, "loc", hop))
    across = flipped(joined, "chan", peers, peers // 2)
    late, again, over = pl.pallas_call(
        functools.partial(late_heads_kernel, split),
        out_shape=(
            jax.ShapeDtypeStruct((own, split, pixel_count), BF16),
            jax.ShapeDtypeStruct((per, features), BF16),
            jax.ShapeDtypeStruct((1,), jnp.int32),
        ),
        in_specs=[VMEM, ANY] + [VMEM] * blocks,
        out_specs=(VMEM, VMEM, SMEM),
        scratch_shapes=turned[:1] + landed[:1],
        compiler_params=vmem,
        cost_estimate=turn_cost,
        name="late_heads",
    )(across, head_weight, *most)
    near = near_rows(joined, across, "chan", peers, again)
    far = flipped(near, "chan", peers, 1)
    rebuilt = pl.pallas_call(
        decode_kernel,
        out_shape=jax.ShapeDtypeStruct((peers, per, own, pixel_count), BF16),
        in_specs=[SMEM] + [VMEM] * 5,
        out_specs=VMEM,
        scratch_shapes=[
            pltpu.VMEM((locations, features), BF16),
            pltpu.VMEM((own, locations, pixel_count), BF16),
        ],
        compiler_params=vmem,
        cost_estimate=pl.CostEstimate(
            flops=2 * locations * features * own * pixel_count,
            bytes_accessed=2 * locations * (features + own * pixel_count),
            transcendentals=0,
        ),
        name="decode",
    )(place, near, far, early, late, head_bias)
    return lax.cond(
        over[0] > 0,
        lambda: plain_shards(
            pixels,
            patch_mask,
            group_map,
            embed_weight,
            mask_token,
            chan_embed,
            agg_weight,
            query_key,
            group_bias,
            norm_gain,
            head_weight,
            head_bias,
        ),
        lambda: rebuilt.reshape(locations, own, pixel_count),
    )


def solution(mesh):
    return jax.shard_map(
        functools.partial(shards, mesh.shape["chan"], mesh.shape["loc"]),
        mesh=mesh,
        in_specs=(
            P("loc", "chan", None),
            P("loc", "chan"),
            P(),
            P(None, "loc"),
            P(),
            P("chan", None),
            P("chan"),
            P(),
            P(),
            P(),
            P(None, "chan", None),
            P("chan", None),
        ),
        out_specs=P("loc", "chan", None),
        check_vma=False,
    )
```

```python
import functools

import jax
import jax.numpy as jnp
from jax import lax
from jax.experimental import pallas as pl
from jax.experimental.pallas import tpu as pltpu
from jax.sharding import PartitionSpec as P

G = 64
BUNDLE = 4
LANES = 128
VMEM = pl.BlockSpec(memory_space=pltpu.VMEM)
SMEM = pl.BlockSpec(memory_space=pltpu.SMEM)
HBM = pl.BlockSpec(memory_space=pltpu.HBM)
ANY = pl.BlockSpec(memory_space=pl.ANY)
F32, BF16 = jnp.float32, jnp.bfloat16


def dot(left, right, left_dim=1, right_dim=0):
    dims = (((left_dim,), (right_dim,)), ((), ()))
    return lax.dot_general(left, right, dims, preferred_element_type=F32)


def iota(shape, axis):
    return lax.broadcasted_iota(jnp.int32, shape, axis)


def halves(value):
    high = value.astype(BF16)
    return high, (value - high.astype(F32)).astype(BF16)


def gelu(value):
    return 0.5 * value * (1.0 + lax.erf(value * 0.7071067811865476))


def slot_tables(group_map):
    bundled = group_map.reshape(-1, BUNDLE)
    lowest = jnp.min(bundled, axis=1)
    highest = jnp.max(bundled, axis=1)
    slot_index = (bundled != lowest[:, None]).astype(jnp.int32)
    choose = slot_index[:, None, :] == jnp.arange(2, dtype=jnp.int32)[None, :, None]
    slot_group = jnp.stack([lowest, highest], axis=1).reshape(-1)
    to_group = jnp.arange(G, dtype=jnp.int32)[:, None] == slot_group[None, :]
    return (choose.astype(BF16), to_group.astype(BF16))


def attend(aggregate, query_key, group_bias, norm_gain):
    rows, _, features = aggregate.shape
    heads = query_key.shape[0]
    high = lax.Precision.HIGHEST
    scores = jnp.einsum("lge,he->lhg", aggregate, query_key.astype(F32), precision=high)
    weights = jax.nn.softmax(scores + group_bias[None], axis=-1)
    split = aggregate.reshape(rows, G, heads, features // heads)
    pooled = jnp.einsum("lhg,lghd->lhd", weights, split, precision=high).reshape(rows, features)
    inverse_rms = lax.rsqrt(jnp.mean(pooled * pooled, axis=-1, keepdims=True) + 1e-06)
    return (pooled * inverse_rms * norm_gain[None]).astype(BF16)


def gathered(value, axis, dim):
    count = lax.axis_size(axis)
    copies = jnp.broadcast_to(value[None], (count,) + value.shape)
    parts = lax.all_to_all(copies, axis, split_axis=0, concat_axis=0, tiled=True)
    parts = jnp.moveaxis(parts, 0, dim)
    return parts.reshape(value.shape[:dim] + (-1,) + value.shape[dim + 1 :])


def plain_join(
    pixels, patch_mask, group_map, embed_weight, mask_token, chan_embed, agg_weight, query_key, group_bias, norm_gain
):
    pixel_count = pixels.shape[2]
    choose, to_group = slot_tables(group_map)
    source_pixels = lax.all_to_all(pixels, "chan", split_axis=0, concat_axis=1, tiled=True)
    source_mask = lax.all_to_all(patch_mask, "chan", split_axis=0, concat_axis=1, tiled=True)
    offsets = gathered(chan_embed, "chan", 0).astype(F32)
    weights = gathered(agg_weight, "chan", 0)
    section = gathered(embed_weight, "loc", 1)
    rows, channels, _ = source_pixels.shape
    features = section.shape[1]
    projected = jnp.dot(source_pixels.reshape(rows * channels, pixel_count), section, preferred_element_type=F32)
    projected = projected.reshape(rows, channels, features)
    hidden = source_mask.reshape(rows, channels, 1) == 1
    pre = jnp.where(hidden, mask_token.astype(F32)[None, None, :], projected) + offsets[None]
    weighted = (jax.nn.gelu(pre, approximate=False) * weights[None, :, None]).astype(BF16)
    bundled = weighted.reshape(rows, channels // BUNDLE, BUNDLE, features)
    sums = jnp.einsum("lbke,bsk->lbse", bundled, choose, preferred_element_type=F32)
    sums = sums.reshape(rows, channels // BUNDLE * 2, features).astype(BF16)
    aggregate = jnp.einsum("gq,lqe->lge", to_group, sums, preferred_element_type=F32)
    return attend(aggregate, query_key, group_bias, norm_gain)


def plain_shards(
    pixels,
    patch_mask,
    group_map,
    embed_weight,
    mask_token,
    chan_embed,
    agg_weight,
    query_key,
    group_bias,
    norm_gain,
    head_weight,
    head_bias,
):
    _, own_channels, pixel_count = pixels.shape
    joined = plain_join(
        pixels, patch_mask, group_map, embed_weight, mask_token, chan_embed, agg_weight, query_key, group_bias, norm_gain
    )
    section = gathered(joined, "chan", 0)
    flat_heads = head_weight.reshape(-1, own_channels * pixel_count)
    decoded = jnp.dot(section, flat_heads, preferred_element_type=F32) + head_bias.reshape(1, -1)
    return decoded.astype(BF16).reshape(section.shape[0], own_channels, pixel_count)


def near_flip(block, count):
    quarter = count // 4
    return block // quarter * (count // 2) + (block + 1) % quarter * 2


def pack_kernel(rows, pixels_ref, mask_ref, weight_ref, out_ref):
    peers, pair_rows, width = pixels_ref.shape
    own, locations = mask_ref.shape
    per = locations // peers
    spread = (iota((own, pair_rows), 1) % own == iota((own, pair_rows), 0)).astype(BF16)
    by_location = dot(mask_ref[...].astype(F32).astype(BF16), spread, 0, 0)
    by_location = by_location.reshape(peers, per, pair_rows)
    keep = iota((1, per, pair_rows), 2) // own == iota((1, per, pair_rows), 1)
    hidden = jnp.sum(jnp.where(keep, by_location, 0.0), axis=1)
    visible = 1.0 - hidden
    before = (iota((pair_rows, pair_rows), 0) < iota((pair_rows, pair_rows), 1)).astype(BF16)
    rank = dot(visible.astype(BF16), before)
    place = jnp.where(visible > 0.5, rank, -1.0)
    limit = float(rows - 2)
    over = jnp.max(place, keepdims=True) >= limit
    marked = hidden + jnp.where(over, 2.0, 0.0)
    weight = weight_ref[...]
    high = weight.astype(BF16)
    middle = (weight - high.astype(F32)).astype(BF16)
    low = (weight - high.astype(F32) - middle.astype(F32)).astype(BF16)
    lane = iota((own, width), 1)
    line = iota((own, width), 0)
    weight_row = jnp.zeros((1, width), F32)
    for part, value in enumerate((high, middle, low)):
        weight_row += dot(value, (lane == line + part * own).astype(BF16))
    index = iota((rows, pair_rows), 0).astype(F32)
    for peer in range(peers):
        chosen = (place[peer : peer + 1, :] == index).astype(BF16)
        packed = dot(chosen, pixels_ref[peer])
        line = iota((rows, width), 0)
        mask_row = jnp.pad(marked[peer : peer + 1, :], ((0, 0), (0, width - pair_rows)))
        packed = jnp.where(line == rows - 2, weight_row, packed)
        packed = jnp.where(line == rows - 1, mask_row, packed)
        out_ref[peer] = packed.astype(BF16)


def fetched_rows(start, steps, head_ref, blocks, arrived):
    depth = blocks.shape[1]

    def fetch(step):
        rows = pl.ds(start + step * depth, depth)
        return pltpu.make_async_copy(head_ref.at[rows], blocks.at[step % 2], arrived.at[step % 2])

    fetch(0).start()
    for step in range(steps):
        if step + 1 < steps:
            fetch(step + 1).start()
        fetch(step).wait()
        yield step, blocks[step % 2]


def early_heads_kernel(start, head_ref, out_ref, blocks, turned, arrived, left):
    depth = blocks.shape[1]
    steps = out_ref.shape[1] // depth

    def store(step):
        rows = pl.ds(step * depth, depth)
        return pltpu.make_async_copy(turned.at[step % 2], out_ref.at[:, rows, :], left.at[step % 2])

    for step, rows in fetched_rows(start, steps, head_ref, blocks, arrived):
        if step >= 2:
            store(step - 2).wait()
        turned[step % 2] = jnp.swapaxes(rows, 0, 1)
        store(step).start()
    for step in range(max(steps - 2, 0), steps):
        store(step).wait()


def late_heads_kernel(start, across_ref, head_ref, *refs):
    *most, out_ref, again_ref, over_ref, blocks, arrived = refs
    over_ref[0] = jnp.max(functools.reduce(jnp.maximum, [ref[...] for ref in most]))
    depth = blocks.shape[1]
    again_ref[...] = across_ref[...]
    for step, rows in fetched_rows(start, out_ref.shape[1] // depth, head_ref, blocks, arrived):
        out_ref[:, step * depth : (step + 1) * depth, :] = jnp.swapaxes(rows, 0, 1)


def join_kernel(
    sizes,
    place_ref,
    packed_ref,
    *refs,
):
    sources, own, per, heads, chunk = sizes
    section_refs = refs[: sizes_sections(refs)]
    rest = refs[len(section_refs) :]
    (chan_ref, other_ref, token_ref, query_ref, group_ref, bias_ref, gain_ref, out_ref, over_ref) = rest[:9]
    (embed, offset, table, choice, where, value, score) = rest[9:]
    _, rows, width = packed_ref.shape
    total = sources * rows
    features = embed.shape[1]
    channels = sources * own
    pair_rows = per * own
    depth = features // heads
    chunks = total // chunk

    me_loc = place_ref[0]
    me = place_ref[1]
    sections = len(section_refs)
    part = features // sections
    for step, section in enumerate(section_refs):
        at = lax.rem(me_loc + step, sections) * part
        embed[:, pl.ds(pl.multiple_of(at, part), part)] = section[...]
    half = sources // 2
    for step in range(half):
        for ref, flip in ((chan_ref, 0), (other_ref, 1)):
            source = jnp.bitwise_xor(me, near_flip(step, sources) + flip)
            offset[pl.ds(pl.multiple_of(source * own, own), own), :] = ref[step * own : (step + 1) * own, :]

    last = [packed_ref[s, rows - 16 :, :].astype(F32) for s in range(sources)]
    marked = jnp.concatenate([tail[15:16, :] for tail in last], axis=0)[:, :pair_rows]
    weight_rows = jnp.concatenate([tail[14:15, :] for tail in last], axis=0)
    over = jnp.max((marked >= 2.0).astype(F32), keepdims=True)
    over_ref[...] = jnp.broadcast_to(over, over_ref.shape).astype(jnp.int32)
    hidden = jnp.where(marked >= 2.0, marked - 2.0, marked)
    visible = 1.0 - hidden
    before = (iota((pair_rows, pair_rows), 0) < iota((pair_rows, pair_rows), 1)).astype(BF16)
    rank = dot(visible.astype(BF16), before)
    place = jnp.where(visible > 0.5, rank, -1.0)
    index = iota((rows, pair_rows), 0).astype(F32)
    of_row = iota((pair_rows, LANES), 0) // own
    to_location = (of_row == iota((pair_rows, LANES), 1)).astype(BF16)
    channel_of_row = iota((pair_rows, channels), 0) % own
    for s in range(sources):
        chosen = (place[s : s + 1, :] == index).astype(BF16)
        to_channel = (channel_of_row + s * own == iota((pair_rows, channels), 1)).astype(BF16)
        choice[s * rows : (s + 1) * rows, :] = dot(chosen, to_channel).astype(BF16)
        where[s * rows : (s + 1) * rows, :] = dot(chosen, to_location).astype(BF16)
    lane = iota((width, channels), 0)
    spread = ((lane % own == iota((width, channels), 1) % own) & (lane < 3 * own)).astype(BF16)
    each = dot(weight_rows.astype(BF16), spread)
    mine = iota((sources, channels), 1) // own == iota((sources, channels), 0)
    weight = jnp.sum(jnp.where(mine, each, 0.0), axis=0, keepdims=True)

    block = 256
    for at in range(0, features, block):
        cols = slice(at, at + block)
        table[:, cols] = gelu(token_ref[:, cols].astype(F32) + offset[:, cols].astype(F32)).astype(BF16)
    table_score = dot(query_ref[...], table[...], 1, 1)

    eye = (iota((per, LANES), 0) == iota((per, LANES), 1)).astype(BF16)
    tile = chunk
    counts = jnp.zeros((per, channels), F32)
    spread_score = jnp.zeros((heads * per, channels), F32)
    for c in range(chunks):
        base = c * chunk
        for at in range(0, features, block):
            cols = slice(at, at + block)
            for top in range(base, base + chunk, tile):
                line = slice(top, top + tile)
                pixel = packed_ref[...].reshape(total, width)[line, :]
                pre = dot(pixel, embed[:, cols]) + dot(choice[line, :], offset[:, cols])
                value[line, cols] = gelu(pre).astype(BF16)
        line = slice(base, base + chunk)
        score[c] = dot(query_ref[...], value[line, :], 1, 1)
        at_location = dot(eye, where[line, :], 1, 1)
        counts += dot(at_location.astype(BF16), choice[line, :])
        by_row = [score[c, h : h + 1, :] * at_location for h in range(heads)]
        for piece in halves(jnp.concatenate(by_row, axis=0)):
            spread_score += dot(piece, choice[line, :])

    hidden_at = 1.0 - counts
    by_row = [hidden_at * table_score[h : h + 1, :] for h in range(heads)]
    full = (spread_score + jnp.concatenate(by_row, axis=0)) * weight
    groups = bias_ref.shape[1]
    to_group = (iota((groups, channels), 0) == group_ref[...]).astype(BF16)
    scores = sum(dot(piece, to_group, 1, 1) for piece in halves(full))
    scores += jnp.concatenate([jnp.broadcast_to(bias_ref[h : h + 1, :], (per, groups)) for h in range(heads)], axis=0)
    scores = jnp.exp(scores - jnp.max(scores, axis=-1, keepdims=True))
    attention = scores / jnp.sum(scores, axis=-1, keepdims=True)
    each = sum(dot(piece, to_group) for piece in halves(attention)) * weight

    of_table = halves(each * jnp.concatenate([hidden_at] * heads, axis=0))
    each = halves(each)
    pooled = [jnp.zeros((2 * per, depth), F32)] * heads

    def stack(pieces, h):
        return jnp.concatenate([piece[h * per : (h + 1) * per, :] for piece in pieces], axis=0)

    for h in range(heads):
        pooled[h] += dot(stack(of_table, h), table[:, h * depth : (h + 1) * depth])
    for c in range(chunks):
        line = slice(c * chunk, (c + 1) * chunk)
        at_location = dot(eye, where[line, :], 1, 1)
        spread_each = sum(dot(piece, choice[line, :], 1, 1) for piece in each)
        pieces = halves(spread_each * jnp.concatenate([at_location] * heads, axis=0))
        for h in range(heads):
            pooled[h] += dot(stack(pieces, h), value[line, h * depth : (h + 1) * depth])
    pooled = [both[:per] + both[per:] for both in pooled]
    square = sum(jnp.sum(rows_of * rows_of, axis=-1, keepdims=True) for rows_of in pooled)
    scale = lax.rsqrt(square * (1.0 / features) + 1e-06)
    for h in range(heads):
        cols = slice(h * depth, (h + 1) * depth)
        out_ref[:, cols] = (pooled[h] * scale * gain_ref[:, cols]).astype(BF16)


def sizes_sections(refs):
    return len(refs) - 16


def decode_kernel(place_ref, near_ref, far_ref, low_ref, high_ref, bias_ref, out_ref, joined, decoded):
    own = bias_ref.shape[0]
    half = near_ref.shape[0]
    count, per = out_ref.shape[:2]
    me = place_ref[1]
    split = low_ref.shape[1]
    joined[:half] = near_ref[...]
    joined[half:] = far_ref[...]
    for c in range(own):
        value = dot(joined[:, :split], low_ref[c]) + dot(joined[:, split:], high_ref[c])
        decoded[c] = (value + bias_ref[c : c + 1, :]).astype(BF16)
    for flip in range(2):
        for step in range(half // per):
            owner = jnp.bitwise_xor(me, near_flip(step, count) + flip)
            top = flip * half + step * per
            out_ref[owner] = jnp.swapaxes(decoded[:, top : top + per, :], 0, 1)


def flipped(value, axis, count, flip):
    return lax.ppermute(value, axis, [(i, i ^ flip) for i in range(count)])


def near_rows(value, across, axis, count, again=None):
    near = []
    for rows, own in ((value, value), (across, across if again is None else again)):
        near += [flipped(rows, axis, count, 2 * k) for k in range(1, count // 4)] + [own]
    return jnp.concatenate(near, axis=0)


def shards(
    peers,
    blocks,
    pixels,
    patch_mask,
    group_map,
    embed_weight,
    mask_token,
    chan_embed,
    agg_weight,
    query_key,
    group_bias,
    norm_gain,
    head_weight,
    head_bias,
):
    locations, own, pixel_count = pixels.shape
    channels = group_map.shape[0]
    heads, features = query_key.shape
    per = locations // peers
    pair_rows = per * own
    rows = -(-pair_rows * 3 // 8 // 16) * 16
    total = peers * rows
    fits = (
        peers & (peers - 1) == 0
        and own % 16 == 0
        and per % 16 == 0
        and pair_rows <= pixel_count
        and 3 * own <= pixel_count
        and total % 512 == 0
    )
    if not fits:
        return plain_shards(
            pixels,
            patch_mask,
            group_map,
            embed_weight,
            mask_token,
            chan_embed,
            agg_weight,
            query_key,
            group_bias,
            norm_gain,
            head_weight,
            head_bias,
        )
    vmem = pltpu.CompilerParams(vmem_limit_bytes=24 << 20)
    place = jnp.stack([lax.axis_index("loc"), lax.axis_index("chan")]).astype(jnp.int32)

    packed = pl.pallas_call(
        functools.partial(pack_kernel, rows),
        out_shape=jax.ShapeDtypeStruct((peers, rows, pixel_count), BF16),
        in_specs=[VMEM] * 3,
        out_specs=VMEM,
        compiler_params=vmem,
        name="pack",
    )(pixels.reshape(peers, pair_rows, pixel_count), patch_mask.T, agg_weight.reshape(1, own))
    packed, sent_weight, sent_embed = lax.optimization_barrier((packed, embed_weight, chan_embed))
    packed = lax.all_to_all(packed, "chan", split_axis=0, concat_axis=0, tiled=True)
    sections = [embed_weight]
    for step in range(1, blocks):
        hop = [(i, (i - step) % blocks) for i in range(blocks)]
        sections.append(lax.ppermute(sent_weight, "loc", hop))
    block = features // 8
    split = 6 * block
    turned = [pltpu.VMEM((2, block, own, pixel_count), BF16), pltpu.VMEM((2, own, block, pixel_count), BF16)]
    landed = [pltpu.SemaphoreType.DMA((2,))] * 2
    turn_cost = pl.CostEstimate(flops=0, bytes_accessed=4 * own * split * pixel_count, transcendentals=0)
    across = flipped(sent_embed, "chan", peers, peers // 2)
    across, sent_head = lax.optimization_barrier((across, head_weight))
    early = pl.pallas_call(
        functools.partial(early_heads_kernel, 0),
        out_shape=pltpu.HBM((own, split, pixel_count), BF16),
        in_specs=[ANY],
        out_specs=HBM,
        scratch_shapes=turned + landed,
        compiler_params=vmem,
        cost_estimate=turn_cost,
        name="early_heads",
    )(sent_head)
    near = near_rows(sent_embed, across, "chan", peers)
    near, early = lax.optimization_barrier((near, early))
    far = flipped(near, "chan", peers, 1)
    chunk = 512
    joined, over = pl.pallas_call(
        functools.partial(join_kernel, (peers, own, per, heads, chunk)),
        out_shape=(
            jax.ShapeDtypeStruct((per, features), BF16),
            jax.ShapeDtypeStruct((8, LANES), jnp.int32),
        ),
        in_specs=[SMEM] + [VMEM] * (8 + blocks),
        out_specs=(VMEM, VMEM),
        scratch_shapes=[
            pltpu.VMEM((pixel_count, features), BF16),
            pltpu.VMEM((channels, features), BF16),
            pltpu.VMEM((channels, features), BF16),
            pltpu.VMEM((total, channels), BF16),
            pltpu.VMEM((total, LANES), BF16),
            pltpu.VMEM((total, features), BF16),
            pltpu.VMEM((total // chunk, heads, chunk), F32),
        ],
        compiler_params=vmem,
        cost_estimate=pl.CostEstimate(
            flops=4 * total * features * (pixel_count + 3 * channels),
            bytes_accessed=2 * features * (pixel_count + channels),
            transcendentals=0,
        ),
        name="join",
    )(
        place,
        packed,
        *sections,
        near,
        far,
        mask_token.reshape(1, features),
        query_key,
        group_map.reshape(1, channels),
        group_bias,
        norm_gain.reshape(1, features),
    )
    most = [over]
    for step in range(1, blocks):
        hop = [(i, (i - step) % blocks) for i in range(blocks)]
        most.append(lax.ppermute(over, "loc", hop))
    across = flipped(joined, "chan", peers, peers // 2)
    late, again, over = pl.pallas_call(
        functools.partial(late_heads_kernel, split),
        out_shape=(
            jax.ShapeDtypeStruct((own, features - split, pixel_count), BF16),
            jax.ShapeDtypeStruct((per, features), BF16),
            jax.ShapeDtypeStruct((1,), jnp.int32),
        ),
        in_specs=[VMEM, ANY] + [VMEM] * blocks,
        out_specs=(VMEM, VMEM, SMEM),
        scratch_shapes=turned[:1] + landed[:1],
        compiler_params=vmem,
        cost_estimate=turn_cost,
        name="late_heads",
    )(across, head_weight, *most)
    near = near_rows(joined, across, "chan", peers, again)
    far = flipped(near, "chan", peers, 1)
    rebuilt = pl.pallas_call(
        decode_kernel,
        out_shape=jax.ShapeDtypeStruct((peers, per, own, pixel_count), BF16),
        in_specs=[SMEM] + [VMEM] * 5,
        out_specs=VMEM,
        scratch_shapes=[
            pltpu.VMEM((locations, features), BF16),
            pltpu.VMEM((own, locations, pixel_count), BF16),
        ],
        compiler_params=vmem,
        cost_estimate=pl.CostEstimate(
            flops=2 * locations * features * own * pixel_count,
            bytes_accessed=2 * locations * (features + own * pixel_count),
            transcendentals=0,
        ),
        name="decode",
    )(place, near, far, early, late, head_bias)
    return lax.cond(
        over[0] > 0,
        lambda: plain_shards(
            pixels,
            patch_mask,
            group_map,
            embed_weight,
            mask_token,
            chan_embed,
            agg_weight,
            query_key,
            group_bias,
            norm_gain,
            head_weight,
            head_bias,
        ),
        lambda: rebuilt.reshape(locations, own, pixel_count),
    )


def solution(mesh):
    return jax.shard_map(
        functools.partial(shards, mesh.shape["chan"], mesh.shape["loc"]),
        mesh=mesh,
        in_specs=(
            P("loc", "chan", None),
            P("loc", "chan"),
            P(),
            P(None, "loc"),
            P(),
            P("chan", None),
            P("chan"),
            P(),
            P(),
            P(),
            P(None, "chan", None),
            P("chan", None),
        ),
        out_specs=P("loc", "chan", None),
        check_vma=False,
    )
```

```python
import functools

import jax
import jax.numpy as jnp
from jax import lax
from jax.experimental import pallas as pl
from jax.experimental.pallas import tpu as pltpu
from jax.sharding import PartitionSpec as P

G = 64
BUNDLE = 4
LANES = 128
VMEM = pl.BlockSpec(memory_space=pltpu.VMEM)
SMEM = pl.BlockSpec(memory_space=pltpu.SMEM)
HBM = pl.BlockSpec(memory_space=pltpu.HBM)
ANY = pl.BlockSpec(memory_space=pl.ANY)
F32, BF16 = jnp.float32, jnp.bfloat16


def dot(left, right, left_dim=1, right_dim=0):
    dims = (((left_dim,), (right_dim,)), ((), ()))
    return lax.dot_general(left, right, dims, preferred_element_type=F32)


def iota(shape, axis):
    return lax.broadcasted_iota(jnp.int32, shape, axis)


def halves(value):
    high = value.astype(BF16)
    return high, (value - high.astype(F32)).astype(BF16)


def gelu(value):
    return 0.5 * value * (1.0 + lax.erf(value * 0.7071067811865476))


def slot_tables(group_map):
    bundled = group_map.reshape(-1, BUNDLE)
    lowest = jnp.min(bundled, axis=1)
    highest = jnp.max(bundled, axis=1)
    slot_index = (bundled != lowest[:, None]).astype(jnp.int32)
    choose = slot_index[:, None, :] == jnp.arange(2, dtype=jnp.int32)[None, :, None]
    slot_group = jnp.stack([lowest, highest], axis=1).reshape(-1)
    to_group = jnp.arange(G, dtype=jnp.int32)[:, None] == slot_group[None, :]
    return (choose.astype(BF16), to_group.astype(BF16))


def attend(aggregate, query_key, group_bias, norm_gain):
    rows, _, features = aggregate.shape
    heads = query_key.shape[0]
    high = lax.Precision.HIGHEST
    scores = jnp.einsum("lge,he->lhg", aggregate, query_key.astype(F32), precision=high)
    weights = jax.nn.softmax(scores + group_bias[None], axis=-1)
    split = aggregate.reshape(rows, G, heads, features // heads)
    pooled = jnp.einsum("lhg,lghd->lhd", weights, split, precision=high).reshape(rows, features)
    inverse_rms = lax.rsqrt(jnp.mean(pooled * pooled, axis=-1, keepdims=True) + 1e-06)
    return (pooled * inverse_rms * norm_gain[None]).astype(BF16)


def gathered(value, axis, dim):
    count = lax.axis_size(axis)
    copies = jnp.broadcast_to(value[None], (count,) + value.shape)
    parts = lax.all_to_all(copies, axis, split_axis=0, concat_axis=0, tiled=True)
    parts = jnp.moveaxis(parts, 0, dim)
    return parts.reshape(value.shape[:dim] + (-1,) + value.shape[dim + 1 :])


def plain_join(
    pixels, patch_mask, group_map, embed_weight, mask_token, chan_embed, agg_weight, query_key, group_bias, norm_gain
):
    pixel_count = pixels.shape[2]
    choose, to_group = slot_tables(group_map)
    source_pixels = lax.all_to_all(pixels, "chan", split_axis=0, concat_axis=1, tiled=True)
    source_mask = lax.all_to_all(patch_mask, "chan", split_axis=0, concat_axis=1, tiled=True)
    offsets = gathered(chan_embed, "chan", 0).astype(F32)
    weights = gathered(agg_weight, "chan", 0)
    section = gathered(embed_weight, "loc", 1)
    rows, channels, _ = source_pixels.shape
    features = section.shape[1]
    projected = jnp.dot(source_pixels.reshape(rows * channels, pixel_count), section, preferred_element_type=F32)
    projected = projected.reshape(rows, channels, features)
    hidden = source_mask.reshape(rows, channels, 1) == 1
    pre = jnp.where(hidden, mask_token.astype(F32)[None, None, :], projected) + offsets[None]
    weighted = (jax.nn.gelu(pre, approximate=False) * weights[None, :, None]).astype(BF16)
    bundled = weighted.reshape(rows, channels // BUNDLE, BUNDLE, features)
    sums = jnp.einsum("lbke,bsk->lbse", bundled, choose, preferred_element_type=F32)
    sums = sums.reshape(rows, channels // BUNDLE * 2, features).astype(BF16)
    aggregate = jnp.einsum("gq,lqe->lge", to_group, sums, preferred_element_type=F32)
    return attend(aggregate, query_key, group_bias, norm_gain)


def plain_shards(
    pixels,
    patch_mask,
    group_map,
    embed_weight,
    mask_token,
    chan_embed,
    agg_weight,
    query_key,
    group_bias,
    norm_gain,
    head_weight,
    head_bias,
):
    _, own_channels, pixel_count = pixels.shape
    joined = plain_join(
        pixels, patch_mask, group_map, embed_weight, mask_token, chan_embed, agg_weight, query_key, group_bias, norm_gain
    )
    section = gathered(joined, "chan", 0)
    flat_heads = head_weight.reshape(-1, own_channels * pixel_count)
    decoded = jnp.dot(section, flat_heads, preferred_element_type=F32) + head_bias.reshape(1, -1)
    return decoded.astype(BF16).reshape(section.shape[0], own_channels, pixel_count)


def near_flip(block, count):
    quarter = count // 4
    return block // quarter * (count // 2) + (block + 1) % quarter * 2


def pack_kernel(rows, pixels_ref, mask_ref, weight_ref, out_ref):
    peers, pair_rows, width = pixels_ref.shape
    own, locations = mask_ref.shape
    per = locations // peers
    spread = (iota((own, pair_rows), 1) % own == iota((own, pair_rows), 0)).astype(BF16)
    by_location = dot(mask_ref[...].astype(F32).astype(BF16), spread, 0, 0)
    by_location = by_location.reshape(peers, per, pair_rows)
    keep = iota((1, per, pair_rows), 2) // own == iota((1, per, pair_rows), 1)
    hidden = jnp.sum(jnp.where(keep, by_location, 0.0), axis=1)
    visible = 1.0 - hidden
    before = (iota((pair_rows, pair_rows), 0) < iota((pair_rows, pair_rows), 1)).astype(BF16)
    rank = dot(visible.astype(BF16), before)
    place = jnp.where(visible > 0.5, rank, -1.0)
    limit = float(rows - 2)
    over = jnp.max(place, keepdims=True) >= limit
    marked = hidden + jnp.where(over, 2.0, 0.0)
    weight = weight_ref[...]
    high = weight.astype(BF16)
    middle = (weight - high.astype(F32)).astype(BF16)
    low = (weight - high.astype(F32) - middle.astype(F32)).astype(BF16)
    lane = iota((own, width), 1)
    line = iota((own, width), 0)
    weight_row = jnp.zeros((1, width), F32)
    for part, value in enumerate((high, middle, low)):
        weight_row += dot(value, (lane == line + part * own).astype(BF16))
    index = iota((rows, pair_rows), 0).astype(F32)
    for peer in range(peers):
        chosen = (place[peer : peer + 1, :] == index).astype(BF16)
        packed = dot(chosen, pixels_ref[peer])
        line = iota((rows, width), 0)
        mask_row = jnp.pad(marked[peer : peer + 1, :], ((0, 0), (0, width - pair_rows)))
        packed = jnp.where(line == rows - 2, weight_row, packed)
        packed = jnp.where(line == rows - 1, mask_row, packed)
        out_ref[peer] = packed.astype(BF16)


def fetched_rows(start, steps, head_ref, blocks, arrived):
    depth = blocks.shape[1]

    def fetch(step):
        rows = pl.ds(start + step * depth, depth)
        return pltpu.make_async_copy(head_ref.at[rows], blocks.at[step % 2], arrived.at[step % 2])

    fetch(0).start()
    for step in range(steps):
        if step + 1 < steps:
            fetch(step + 1).start()
        fetch(step).wait()
        yield step, blocks[step % 2]


def early_heads_kernel(start, head_ref, out_ref, blocks, turned, arrived, left):
    depth = blocks.shape[1]
    steps = out_ref.shape[1] // depth

    def store(step):
        rows = pl.ds(step * depth, depth)
        return pltpu.make_async_copy(turned.at[step % 2], out_ref.at[:, rows, :], left.at[step % 2])

    for step, rows in fetched_rows(start, steps, head_ref, blocks, arrived):
        if step >= 2:
            store(step - 2).wait()
        turned[step % 2] = jnp.swapaxes(rows, 0, 1)
        store(step).start()
    for step in range(max(steps - 2, 0), steps):
        store(step).wait()


def late_heads_kernel(start, across_ref, head_ref, *refs):
    *most, out_ref, again_ref, over_ref, blocks, arrived = refs
    over_ref[0] = jnp.max(functools.reduce(jnp.maximum, [ref[...] for ref in most]))
    depth = blocks.shape[1]
    again_ref[...] = across_ref[...]
    for step, rows in fetched_rows(start, out_ref.shape[1] // depth, head_ref, blocks, arrived):
        out_ref[:, step * depth : (step + 1) * depth, :] = jnp.swapaxes(rows, 0, 1)


def join_kernel(
    sizes,
    place_ref,
    packed_ref,
    *refs,
):
    sources, own, per, heads, chunk = sizes
    section_refs = refs[: sizes_sections(refs)]
    rest = refs[len(section_refs) :]
    (chan_ref, other_ref, token_ref, query_ref, group_ref, bias_ref, gain_ref, out_ref, over_ref) = rest[:9]
    (embed, offset, table, choice, where, value, score) = rest[9:]
    _, rows, width = packed_ref.shape
    total = sources * rows
    features = embed.shape[1]
    channels = sources * own
    pair_rows = per * own
    depth = features // heads
    chunks = total // chunk

    me_loc = place_ref[0]
    me = place_ref[1]
    sections = len(section_refs)
    part = features // sections
    for step, section in enumerate(section_refs):
        at = lax.rem(me_loc + step, sections) * part
        embed[:, pl.ds(pl.multiple_of(at, part), part)] = section[...]
    half = sources // 2
    for step in range(half):
        for ref, flip in ((chan_ref, 0), (other_ref, 1)):
            source = jnp.bitwise_xor(me, near_flip(step, sources) + flip)
            offset[pl.ds(pl.multiple_of(source * own, own), own), :] = ref[step * own : (step + 1) * own, :]

    last = [packed_ref[s, rows - 16 :, :].astype(F32) for s in range(sources)]
    marked = jnp.concatenate([tail[15:16, :] for tail in last], axis=0)[:, :pair_rows]
    weight_rows = jnp.concatenate([tail[14:15, :] for tail in last], axis=0)
    over = jnp.max((marked >= 2.0).astype(F32), keepdims=True)
    over_ref[...] = jnp.broadcast_to(over, over_ref.shape).astype(jnp.int32)
    hidden = jnp.where(marked >= 2.0, marked - 2.0, marked)
    visible = 1.0 - hidden
    before = (iota((pair_rows, pair_rows), 0) < iota((pair_rows, pair_rows), 1)).astype(BF16)
    rank = dot(visible.astype(BF16), before)
    place = jnp.where(visible > 0.5, rank, -1.0)
    index = iota((rows, pair_rows), 0).astype(F32)
    of_row = iota((pair_rows, LANES), 0) // own
    to_location = (of_row == iota((pair_rows, LANES), 1)).astype(BF16)
    channel_of_row = iota((pair_rows, channels), 0) % own
    for s in range(sources):
        chosen = (place[s : s + 1, :] == index).astype(BF16)
        to_channel = (channel_of_row + s * own == iota((pair_rows, channels), 1)).astype(BF16)
        choice[s * rows : (s + 1) * rows, :] = dot(chosen, to_channel).astype(BF16)
        where[s * rows : (s + 1) * rows, :] = dot(chosen, to_location).astype(BF16)
    lane = iota((width, channels), 0)
    spread = ((lane % own == iota((width, channels), 1) % own) & (lane < 3 * own)).astype(BF16)
    each = dot(weight_rows.astype(BF16), spread)
    mine = iota((sources, channels), 1) // own == iota((sources, channels), 0)
    weight = jnp.sum(jnp.where(mine, each, 0.0), axis=0, keepdims=True)

    block = 256
    for at in range(0, features, block):
        cols = slice(at, at + block)
        table[:, cols] = gelu(token_ref[:, cols].astype(F32) + offset[:, cols].astype(F32)).astype(BF16)
    table_score = dot(query_ref[...], table[...], 1, 1)

    eye = (iota((per, LANES), 0) == iota((per, LANES), 1)).astype(BF16)
    tile = chunk
    counts = jnp.zeros((per, channels), F32)
    spread_score = jnp.zeros((heads * per, channels), F32)
    for c in range(chunks):
        base = c * chunk
        for at in range(0, features, block):
            cols = slice(at, at + block)
            for top in range(base, base + chunk, tile):
                line = slice(top, top + tile)
                pixel = packed_ref[...].reshape(total, width)[line, :]
                pre = dot(pixel, embed[:, cols]) + dot(choice[line, :], offset[:, cols])
                value[line, cols] = gelu(pre).astype(BF16)
        line = slice(base, base + chunk)
        score[c] = dot(query_ref[...], value[line, :], 1, 1)
        at_location = dot(eye, where[line, :], 1, 1)
        counts += dot(at_location.astype(BF16), choice[line, :])
        by_row = [score[c, h : h + 1, :] * at_location for h in range(heads)]
        for piece in halves(jnp.concatenate(by_row, axis=0)):
            spread_score += dot(piece, choice[line, :])

    hidden_at = 1.0 - counts
    by_row = [hidden_at * table_score[h : h + 1, :] for h in range(heads)]
    full = (spread_score + jnp.concatenate(by_row, axis=0)) * weight
    groups = bias_ref.shape[1]
    to_group = (iota((groups, channels), 0) == group_ref[...]).astype(BF16)
    scores = sum(dot(piece, to_group, 1, 1) for piece in halves(full))
    scores += jnp.concatenate([jnp.broadcast_to(bias_ref[h : h + 1, :], (per, groups)) for h in range(heads)], axis=0)
    scores = jnp.exp(scores - jnp.max(scores, axis=-1, keepdims=True))
    attention = scores / jnp.sum(scores, axis=-1, keepdims=True)
    each = sum(dot(piece, to_group) for piece in halves(attention)) * weight

    of_table = halves(each * jnp.concatenate([hidden_at] * heads, axis=0))
    each = halves(each)
    pooled = [jnp.zeros((2 * per, depth), F32)] * heads

    def stack(pieces, h):
        return jnp.concatenate([piece[h * per : (h + 1) * per, :] for piece in pieces], axis=0)

    for h in range(heads):
        pooled[h] += dot(stack(of_table, h), table[:, h * depth : (h + 1) * depth])
    for c in range(chunks):
        line = slice(c * chunk, (c + 1) * chunk)
        at_location = dot(eye, where[line, :], 1, 1)
        spread_each = sum(dot(piece, choice[line, :], 1, 1) for piece in each)
        pieces = halves(spread_each * jnp.concatenate([at_location] * heads, axis=0))
        for h in range(heads):
            pooled[h] += dot(stack(pieces, h), value[line, h * depth : (h + 1) * depth])
    pooled = [both[:per] + both[per:] for both in pooled]
    square = sum(jnp.sum(rows_of * rows_of, axis=-1, keepdims=True) for rows_of in pooled)
    scale = lax.rsqrt(square * (1.0 / features) + 1e-06)
    for h in range(heads):
        cols = slice(h * depth, (h + 1) * depth)
        out_ref[:, cols] = (pooled[h] * scale * gain_ref[:, cols]).astype(BF16)


def sizes_sections(refs):
    return len(refs) - 16


def decode_kernel(place_ref, near_ref, far_ref, low_ref, high_ref, bias_ref, out_ref, joined, decoded):
    own = bias_ref.shape[0]
    half = near_ref.shape[0]
    count, per = out_ref.shape[:2]
    me = place_ref[1]
    split = low_ref.shape[1]
    joined[:half] = near_ref[...]
    joined[half:] = far_ref[...]
    for c in range(own):
        value = dot(joined[:, :split], low_ref[c]) + dot(joined[:, split:], high_ref[c])
        decoded[c] = (value + bias_ref[c : c + 1, :]).astype(BF16)
    for flip in range(2):
        for step in range(half // per):
            owner = jnp.bitwise_xor(me, near_flip(step, count) + flip)
            top = flip * half + step * per
            out_ref[owner] = jnp.swapaxes(decoded[:, top : top + per, :], 0, 1)


def flipped(value, axis, count, flip):
    return lax.ppermute(value, axis, [(i, i ^ flip) for i in range(count)])


def near_rows(value, across, axis, count, again=None):
    near = []
    for rows, own in ((value, value), (across, across if again is None else again)):
        near += [flipped(rows, axis, count, 2 * k) for k in range(1, count // 4)] + [own]
    return jnp.concatenate(near, axis=0)


def shards(
    peers,
    blocks,
    pixels,
    patch_mask,
    group_map,
    embed_weight,
    mask_token,
    chan_embed,
    agg_weight,
    query_key,
    group_bias,
    norm_gain,
    head_weight,
    head_bias,
):
    locations, own, pixel_count = pixels.shape
    channels = group_map.shape[0]
    heads, features = query_key.shape
    per = locations // peers
    pair_rows = per * own
    rows = -(-pair_rows * 3 // 8 // 16) * 16
    total = peers * rows
    fits = (
        peers & (peers - 1) == 0
        and own % 16 == 0
        and per % 16 == 0
        and pair_rows <= pixel_count
        and 3 * own <= pixel_count
        and total % 512 == 0
    )
    if not fits:
        return plain_shards(
            pixels,
            patch_mask,
            group_map,
            embed_weight,
            mask_token,
            chan_embed,
            agg_weight,
            query_key,
            group_bias,
            norm_gain,
            head_weight,
            head_bias,
        )
    vmem = pltpu.CompilerParams(vmem_limit_bytes=24 << 20)
    place = jnp.stack([lax.axis_index("loc"), lax.axis_index("chan")]).astype(jnp.int32)

    packed = pl.pallas_call(
        functools.partial(pack_kernel, rows),
        out_shape=jax.ShapeDtypeStruct((peers, rows, pixel_count), BF16),
        in_specs=[VMEM] * 3,
        out_specs=VMEM,
        compiler_params=vmem,
        name="pack",
    )(pixels.reshape(peers, pair_rows, pixel_count), patch_mask.T, agg_weight.reshape(1, own))
    packed, sent_weight, sent_embed = lax.optimization_barrier((packed, embed_weight, chan_embed))
    packed = lax.all_to_all(packed, "chan", split_axis=0, concat_axis=0, tiled=True)
    sections = [embed_weight]
    for step in range(1, blocks):
        hop = [(i, (i - step) % blocks) for i in range(blocks)]
        sections.append(lax.ppermute(sent_weight, "loc", hop))
    block = features // 8
    split = 6 * block
    turned = [pltpu.VMEM((2, block, own, pixel_count), BF16), pltpu.VMEM((2, own, block, pixel_count), BF16)]
    landed = [pltpu.SemaphoreType.DMA((2,))] * 2
    turn_cost = pl.CostEstimate(flops=0, bytes_accessed=4 * own * split * pixel_count, transcendentals=0)
    across = flipped(sent_embed, "chan", peers, peers // 2)
    across, sent_head = lax.optimization_barrier((across, head_weight))
    early = pl.pallas_call(
        functools.partial(early_heads_kernel, 0),
        out_shape=pltpu.HBM((own, split, pixel_count), BF16),
        in_specs=[ANY],
        out_specs=HBM,
        scratch_shapes=turned + landed,
        compiler_params=vmem,
        cost_estimate=turn_cost,
        name="early_heads",
    )(sent_head)
    near = near_rows(sent_embed, across, "chan", peers)
    near, early = lax.optimization_barrier((near, early))
    far = flipped(near, "chan", peers, 1)
    chunk = total // 2
    joined, over = pl.pallas_call(
        functools.partial(join_kernel, (peers, own, per, heads, chunk)),
        out_shape=(
            jax.ShapeDtypeStruct((per, features), BF16),
            jax.ShapeDtypeStruct((8, LANES), jnp.int32),
        ),
        in_specs=[SMEM] + [VMEM] * (8 + blocks),
        out_specs=(VMEM, VMEM),
        scratch_shapes=[
            pltpu.VMEM((pixel_count, features), BF16),
            pltpu.VMEM((channels, features), BF16),
            pltpu.VMEM((channels, features), BF16),
            pltpu.VMEM((total, channels), BF16),
            pltpu.VMEM((total, LANES), BF16),
            pltpu.VMEM((total, features), BF16),
            pltpu.VMEM((total // chunk, heads, chunk), F32),
        ],
        compiler_params=vmem,
        cost_estimate=pl.CostEstimate(
            flops=4 * total * features * (pixel_count + 3 * channels),
            bytes_accessed=2 * features * (pixel_count + channels),
            transcendentals=0,
        ),
        name="join",
    )(
        place,
        packed,
        *sections,
        near,
        far,
        mask_token.reshape(1, features),
        query_key,
        group_map.reshape(1, channels),
        group_bias,
        norm_gain.reshape(1, features),
    )
    most = [over]
    for step in range(1, blocks):
        hop = [(i, (i - step) % blocks) for i in range(blocks)]
        most.append(lax.ppermute(over, "loc", hop))
    across = flipped(joined, "chan", peers, peers // 2)
    late, again, over = pl.pallas_call(
        functools.partial(late_heads_kernel, split),
        out_shape=(
            jax.ShapeDtypeStruct((own, features - split, pixel_count), BF16),
            jax.ShapeDtypeStruct((per, features), BF16),
            jax.ShapeDtypeStruct((1,), jnp.int32),
        ),
        in_specs=[VMEM, ANY] + [VMEM] * blocks,
        out_specs=(VMEM, VMEM, SMEM),
        scratch_shapes=turned[:1] + landed[:1],
        compiler_params=vmem,
        cost_estimate=turn_cost,
        name="late_heads",
    )(across, head_weight, *most)
    near = near_rows(joined, across, "chan", peers, again)
    far = flipped(near, "chan", peers, 1)
    rebuilt = pl.pallas_call(
        decode_kernel,
        out_shape=jax.ShapeDtypeStruct((peers, per, own, pixel_count), BF16),
        in_specs=[SMEM] + [VMEM] * 5,
        out_specs=VMEM,
        scratch_shapes=[
            pltpu.VMEM((locations, features), BF16),
            pltpu.VMEM((own, locations, pixel_count), BF16),
        ],
        compiler_params=vmem,
        cost_estimate=pl.CostEstimate(
            flops=2 * locations * features * own * pixel_count,
            bytes_accessed=2 * locations * (features + own * pixel_count),
            transcendentals=0,
        ),
        name="decode",
    )(place, near, far, early, late, head_bias)
    return lax.cond(
        over[0] > 0,
        lambda: plain_shards(
            pixels,
            patch_mask,
            group_map,
            embed_weight,
            mask_token,
            chan_embed,
            agg_weight,
            query_key,
            group_bias,
            norm_gain,
            head_weight,
            head_bias,
        ),
        lambda: rebuilt.reshape(locations, own, pixel_count),
    )


def solution(mesh):
    return jax.shard_map(
        functools.partial(shards, mesh.shape["chan"], mesh.shape["loc"]),
        mesh=mesh,
        in_specs=(
            P("loc", "chan", None),
            P("loc", "chan"),
            P(),
            P(None, "loc"),
            P(),
            P("chan", None),
            P("chan"),
            P(),
            P(),
            P(),
            P(None, "chan", None),
            P("chan", None),
        ),
        out_specs=P("loc", "chan", None),
        check_vma=False,
    )
```
